32 devices in a mesh: seq: 8 (over z, y), mp: 4 (over x, core).
Axes of the slice: x: 2, y: 2, z: 4, core: 2. Of those that a mesh axis runs over, the one named last changes fastest.
Arguments:
- out_grad: bfloat16 [4096, 8192], P('seq', 'mp'), may hold values from -6 to 6
- out_weight: bfloat16 [4096, 8192], P('mp'), may hold values from -0.0625 to 0.0625
- queries: bfloat16 [4096, 4096], P('seq', 'mp'), may hold values from -5 to 5
- keys: bfloat16 [16, 128, 4096], P('seq', None, 'mp'), may hold values from -5 to 5
- values: bfloat16 [16, 128, 4096], P('seq', None, 'mp'), may hold values from -6 to 6
- retrieval: int32 [64, 2], replicated, may hold values from 0 to 15, as said below
- counts: int32 [64], P('seq'), may hold values from 1 to 2
Outputs:
- query_grad: bfloat16 [4096, 4096], P('seq', 'mp')
- key_grad: bfloat16 [16, 128, 4096], P('seq', None, 'mp')
- value_grad: bfloat16 [16, 128, 4096], P('seq', None, 'mp')
The draws below stay inside these ranges and needn't reach their ends.
Inputs may be any that keep to these rules, and one draw needn't show every extreme that they name: `retrieval`: entry e is held by index e // 2 of seq. The 16 neighbour places of one index's blocks name entries of any one owner at most 2 times, and some owner is named exactly 2 times by the blocks of every index.
All inputs are finite; a program needn't handle non-finite values.
Results may differ from the reference program's by a relative error of at most 0.0091.
Values may be sent and summed in bfloat16 or wider, within the bound.
No kernel may reach another device: no remote copies, remote signals or barrier semaphores. Data moves between devices by JAX's collectives and lax.ppermute only.
A program may use at most 128 MiB of HBM per device.

```python
import math
import jax
import jax.numpy as jnp
from jax import lax

D = 8192
HEADS = 32
HEAD = 128
BLOCK = 64
NEIGH = 2
NROW = 128
TOK_DEV = 512
NEI_DEV = 2
TOKENS = 4096
CH_DEV = 8
BLOCKS = 64
SLOTS_DEV = 16
CAP = 2
ENTRIES = 16
N_SEQ = 8


def draw_queries(key, part):
    shape = (TOK_DEV * N_SEQ, HEADS * HEAD)
    own_key = jax.random.fold_in(key, 1)
    result = jax.random.truncated_normal(own_key, -5.0, 5.0, shape, jnp.float32)
    return result.astype(jnp.bfloat16)


def draw_keys(key, part):
    shape = (NEI_DEV * N_SEQ, NROW, HEADS * HEAD)
    own_key = jax.random.fold_in(key, 2)
    result = jax.random.truncated_normal(own_key, -5.0, 5.0, shape, jnp.float32)
    return result.astype(jnp.bfloat16)


def draw_retrieval(key, part):
    readers = BLOCKS // CH_DEV
    slot_total = SLOTS_DEV
    slot_cap = CAP
    hot_owner = jax.random.randint(jax.random.fold_in(key, 11), (), 0, readers)

    def other_order(sub_key):
        return jax.random.permutation(sub_key, readers - 1)

    def slot_order(sub_key):
        return jax.random.permutation(sub_key, slot_total)
    others = jax.vmap(other_order)(jax.random.split(jax.random.fold_in(key, 12), readers))
    place = jnp.arange(slot_total)
    spread = max(slot_total - slot_cap, 1)
    group = jnp.where(place < slot_cap, 0, 1 + (place - slot_cap) * (readers - 1) // spread)
    group_index = jnp.broadcast_to(jnp.maximum(group - 1, 0)[None, :], (readers, slot_total))
    picked = jnp.take_along_axis(others, group_index, axis=1)
    owners = jnp.where(group[None, :] == 0, hot_owner, (hot_owner + 1 + picked) % readers)
    shuffles = jax.vmap(slot_order)(jax.random.split(jax.random.fold_in(key, 13), readers))
    owners = jnp.take_along_axis(owners, shuffles, axis=1)
    local_ids = jax.random.randint(jax.random.fold_in(key, 14), (readers, slot_total), 0, NEI_DEV)
    return (owners * NEI_DEV + local_ids).reshape(BLOCKS, NEIGH).astype(jnp.int32)


def with_ends(values, key, least, largest):
    longest = values.shape.index(max(values.shape))
    spots = []
    for shift in (0, 1):
        where = [jax.random.randint(jax.random.fold_in(key, axis), (), 0, length) for axis, length in enumerate(values.shape)]
        where[longest] = (where[longest] + shift) % values.shape[longest]
        spots.append(tuple(where))
    return values.at[spots[0]].set(least).at[spots[1]].set(largest)


def block_scale(rng, shape, cuts, low, largest):
    def one(axis_at, parts):
        steps = jax.random.uniform(jax.random.fold_in(jax.random.fold_in(rng, 6), axis_at), (parts,), jnp.float32, low / len(cuts), largest / len(cuts))
        return jnp.repeat(jnp.exp(steps), shape[axis_at] // parts).reshape((-1,) + (1,) * (len(shape) - axis_at - 1))

    gain = one(*cuts[0])
    for cut in cuts[1:]:
        gain = gain * one(*cut)
    return gain


def noise(stream_key, shape, deviation, bound, cuts=(), held_as=jnp.bfloat16):
    factor_of = block_scale(stream_key, shape, cuts, -0.22, 0.18) if cuts else 1.0
    array = jax.random.normal(stream_key, shape, jnp.float32) * deviation * factor_of
    return jnp.minimum(jnp.maximum(array, -bound), bound).astype(held_as)


def setup_inputs(seed: int = 0) -> dict:
    key_of = jax.random.split(jax.random.key(seed), 8)
    return {
        "out_grad": noise(key_of[0], (TOKENS, D), 1.0, 6.0, ((0, 8), (1, 4))),
        "out_weight": noise(key_of[1], (HEADS * HEAD, D), D ** -0.5, 0.0625, ((0, 4),)),
        "queries": draw_queries(jax.random.fold_in(key_of[7], 71), 0),
        "keys": draw_keys(jax.random.fold_in(key_of[7], 71), 0),
        "values": noise(key_of[4], (ENTRIES, NROW, HEADS * HEAD), 1.0, 6.0, ((0, 8), (2, 4))),
        "retrieval": draw_retrieval(jax.random.fold_in(key_of[7], 71), 0),
        "counts": with_ends(jax.random.randint(key_of[6], (BLOCKS,), 1, NEIGH + 1), jax.random.fold_in(key_of[6], 1), 1, NEIGH).astype(jnp.int32),
    }


def block_terms(query_rows, grad_rows, key_rows, value_rows, live_keys):
    score_scale = 1.0 / math.sqrt(HEAD)
    scores = jnp.einsum('qhe,khe->hqk', query_rows.astype(jnp.float32), key_rows.astype(jnp.float32)) * score_scale
    live_mask = live_keys[None, None, :]
    row_max = lax.optimization_barrier(jnp.max(jnp.where(live_mask, scores, -jnp.inf), axis=-1, keepdims=True))
    raised = jnp.where(live_mask, jnp.exp(scores - row_max), 0.0)
    attn_weights = raised / lax.optimization_barrier(jnp.sum(raised, axis=-1, keepdims=True))
    weights_low = attn_weights.astype(jnp.bfloat16)
    attn_out = jnp.einsum('hqk,khe->qhe', weights_low.astype(jnp.float32), value_rows.astype(jnp.float32))
    row_dot = lax.optimization_barrier(jnp.sum(grad_rows.astype(jnp.float32) * attn_out, axis=-1))
    grad_weights = jnp.einsum('qhe,khe->hqk', grad_rows.astype(jnp.float32), value_rows.astype(jnp.float32))
    grad_scores = attn_weights * (grad_weights - jnp.transpose(row_dot, (1, 0))[:, :, None])
    grad_low = grad_scores.astype(jnp.bfloat16).astype(jnp.float32)
    query_grad = (jnp.einsum('hqk,khe->qhe', grad_low, key_rows.astype(jnp.float32)) * score_scale).astype(jnp.bfloat16)
    key_terms = (jnp.einsum('hqk,qhe->khe', grad_low, query_rows.astype(jnp.float32)) * score_scale).astype(jnp.bfloat16)
    value_terms = jnp.einsum('hqk,qhe->khe', weights_low.astype(jnp.float32), grad_rows.astype(jnp.float32)).astype(jnp.bfloat16)
    return (query_grad, key_terms, value_terms)

def reference(out_grad, out_weight, queries, keys, values, retrieval, counts):
    head_cols = HEADS * HEAD
    grad_out = jnp.dot(out_grad, out_weight.T, preferred_element_type=jnp.float32).astype(jnp.bfloat16)
    query_view = queries.reshape(BLOCKS, BLOCK, HEADS, HEAD)
    grad_view = grad_out.reshape(BLOCKS, BLOCK, HEADS, HEAD)

    def step_fn(carry, inputs):
        key_acc, value_acc = carry
        query_rows, grad_rows, lists, count_now = inputs
        key_rows = jnp.take(keys, lists, axis=0).reshape(NEIGH * NROW, HEADS, HEAD)
        value_rows = jnp.take(values, lists, axis=0).reshape(NEIGH * NROW, HEADS, HEAD)
        live_keys = jnp.arange(NEIGH * NROW, dtype=jnp.int32) < count_now * NROW
        query_grad, key_terms, value_terms = block_terms(query_rows, grad_rows, key_rows, value_rows, live_keys)
        key_acc = key_acc.at[lists].add(key_terms.reshape(NEIGH, NROW, head_cols).astype(jnp.float32))
        value_acc = value_acc.at[lists].add(value_terms.reshape(NEIGH, NROW, head_cols).astype(jnp.float32))
        return ((key_acc, value_acc), query_grad)
    start_acc = (jnp.zeros((ENTRIES, NROW, head_cols), jnp.float32), jnp.zeros((ENTRIES, NROW, head_cols), jnp.float32))
    final_acc, query_grads = lax.scan(step_fn, start_acc, (query_view, grad_view, retrieval, counts))
    key_acc, value_acc = final_acc
    return (query_grads.reshape(TOKENS, head_cols), key_acc.astype(jnp.bfloat16), value_acc.astype(jnp.bfloat16))
```

```python
import functools
import math

import jax
import jax.numpy as jnp
from jax import lax
from jax.experimental import pallas as pl
from jax.experimental.pallas import tpu as pltpu
from jax.sharding import PartitionSpec as P

HEAD = 128
BLOCK = 64
NEIGH = 2
LANES = 128
HEAD_CHUNKS = 2
F32 = jnp.float32
BF16 = jnp.bfloat16


def vmem_params(flops=0, moved=0):
    return dict(
        compiler_params=pltpu.CompilerParams(vmem_limit_bytes=48 * 1024 * 1024),
        cost_estimate=pl.CostEstimate(flops=flops, bytes_accessed=moved, transcendentals=0),
    )


def slot_of_place(lists_ref, base, place, entries_here, slot_cap):
    owner = lists_ref[base + place] // entries_here
    rank = 0
    for earlier in range(place):
        rank = rank + jnp.where(lists_ref[base + earlier] // entries_here == owner, 1, 0)
    return owner * slot_cap + rank


def place_rows(rows, lists_flat, my_index, n_seq, slot_cap, entries_here):
    tok_rows, cols = rows.shape
    places = tok_rows // BLOCK * NEIGH
    slots = n_seq * slot_cap

    def body(lists_ref, index_ref, rows_ref, out_ref, zero_ref, sems):
        base = index_ref[0] * places
        if slots > places:
            zero_ref[...] = jnp.zeros_like(zero_ref)
            for slot in range(slots):
                pltpu.make_async_copy(zero_ref, out_ref.at[slot], sems.at[slot]).start()
            for slot in range(slots):
                pltpu.make_async_copy(zero_ref, out_ref.at[slot], sems.at[slot]).wait()
        copies = []
        for place in range(places):
            slot = slot_of_place(lists_ref, base, place, entries_here, slot_cap)
            start = place // NEIGH * BLOCK
            copies.append(
                pltpu.make_async_copy(
                    rows_ref.at[pl.ds(start, BLOCK)], out_ref.at[slot], sems.at[place]
                )
            )
            copies[-1].start()
        for copy in copies:
            copy.wait()

    return pl.pallas_call(
        body,
        out_shape=jax.ShapeDtypeStruct((slots, BLOCK, cols), rows.dtype),
        in_specs=[
            pl.BlockSpec(memory_space=pltpu.SMEM),
            pl.BlockSpec(memory_space=pltpu.SMEM),
            pl.BlockSpec(memory_space=pl.ANY),
        ],
        out_specs=pl.BlockSpec(memory_space=pl.ANY),
        scratch_shapes=[
            pltpu.VMEM((BLOCK, cols), rows.dtype),
            pltpu.SemaphoreType.DMA((max(slots, places),)),
        ],
        name="place_rows",
        **vmem_params(moved=2 * slots * BLOCK * cols * 2),
    )(lists_flat, my_index, rows)


def join_places(back, lists_flat, my_index, n_seq, slot_cap, entries_here, blocks_here):
    slots, _, cols = back.shape
    places = blocks_here * NEIGH

    def body(lists_ref, index_ref, back_ref, out_ref):
        base = index_ref[0] * places
        for block in range(blocks_here):
            total = 0.0
            for neighbour in range(NEIGH):
                slot = slot_of_place(
                    lists_ref, base, block * NEIGH + neighbour, entries_here, slot_cap
                )
                total = total + back_ref[slot].astype(F32)
            out_ref[block * BLOCK : (block + 1) * BLOCK, :] = total.astype(out_ref.dtype)

    return pl.pallas_call(
        body,
        out_shape=jax.ShapeDtypeStruct((blocks_here * BLOCK, cols), back.dtype),
        in_specs=[
            pl.BlockSpec(memory_space=pltpu.SMEM),
            pl.BlockSpec(memory_space=pltpu.SMEM),
            pl.BlockSpec(memory_space=pltpu.VMEM),
        ],
        out_specs=pl.BlockSpec(memory_space=pltpu.VMEM),
        name="join_places",
        **vmem_params(moved=3 * slots * BLOCK * cols),
    )(lists_flat, my_index, back)


def lane_parts(total):
    width = 256 if total % 256 == 0 else LANES
    return [slice(at, at + width) for at in range(0, total, width)]


def pick_entry(stacked, entry):
    entries = stacked.shape[0] // LANES
    chosen = stacked[:LANES]
    for number in range(1, entries):
        chosen = jnp.where(
            entry == number, stacked[number * LANES : (number + 1) * LANES], chosen
        )
    return chosen


def spread_entry(chosen, entry, entries):
    return jnp.concatenate(
        [jnp.where(entry == number, chosen, 0.0) for number in range(entries)], axis=0
    ).astype(BF16)


NT = (((1,), (1,)), ((), ()))
NN = (((1,), (0,)), ((), ()))
TN = (((0,), (0,)), ((), ()))


def local_softmax(query_rows, keys, entry_lanes):
    rows, cols = query_rows.shape
    heads = cols // HEAD
    key_rows = keys.shape[0]
    scale = 1.0 / math.sqrt(HEAD)

    def body(query_ref, key_ref, entry_ref, weight_ref, lse_ref):
        head = pl.program_id(0)
        for part in lane_parts(rows):
            entry = entry_ref[:, part]
            scores = lax.dot_general(
                key_ref[...], query_ref[part, :], NT, preferred_element_type=F32
            )
            scores = pick_entry(scores, entry) * scale
            top = jnp.max(scores, axis=0, keepdims=True)
            raised = jnp.exp(scores - top)
            total = jnp.sum(raised, axis=0, keepdims=True)
            weight_ref[0, :, part] = raised / total
            lse_ref[pl.ds(head, 1), part] = top + jnp.log(total)

    return pl.pallas_call(
        body,
        grid=(heads,),
        out_shape=(
            jax.ShapeDtypeStruct((heads, LANES, rows), F32),
            jax.ShapeDtypeStruct((heads, rows), F32),
        ),
        in_specs=[
            pl.BlockSpec((rows, HEAD), lambda h: (0, h)),
            pl.BlockSpec((key_rows, HEAD), lambda h: (0, h)),
            pl.BlockSpec((1, rows), lambda h: (0, 0)),
        ],
        out_specs=(
            pl.BlockSpec((1, LANES, rows), lambda h: (h, 0, 0)),
            pl.BlockSpec((heads, rows), lambda h: (0, 0)),
        ),
        name="local_softmax",
        **vmem_params(2 * rows * key_rows * cols, 6 * heads * LANES * rows),
    )(query_rows, keys, entry_lanes)


def partner_lanes(partner_ref, all_ref, out_ref, slots):
    heads = out_ref.shape[0]
    lane = lax.broadcasted_iota(jnp.int32, (heads, LANES), 1)
    for group in range(slots // 2):
        halves = []
        for half in range(2):
            slot = group * 2 + half
            device, there = partner_ref[0, slot], partner_ref[1, slot]
            start = pl.multiple_of(there // 2 * LANES, LANES)
            tile = all_ref[device, :, pl.ds(start, LANES)]
            turned = pltpu.roll(tile, BLOCK, 1)
            halves.append(jnp.where(there % 2 == half, tile, turned))
        out_ref[:, group * LANES : (group + 1) * LANES] = jnp.where(
            lane < BLOCK, halves[0], halves[1]
        )


def weight_grads(
    chunk, weights, lse, all_lse, partner, live_lanes, grad_rows, values, entry_lanes
):
    heads, _, rows = weights.shape
    here = grad_rows.shape[1] // HEAD
    first = chunk * here
    value_rows = values.shape[0]
    slots = rows // BLOCK
    devices = all_lse.shape[0]

    def body(
        partner_ref,
        weight_ref,
        lse_ref,
        all_ref,
        live_ref,
        grad_ref,
        value_ref,
        entry_ref,
        slope_ref,
        share_ref,
        dot_ref,
        other_ref,
    ):
        head = pl.program_id(0)

        @pl.when(head == 0)
        def _():
            partner_lanes(partner_ref, all_ref, other_ref, slots)

        for part in lane_parts(rows):
            entry = entry_ref[:, part]
            own = lse_ref[pl.ds(first + head, 1), part]
            other = other_ref[pl.ds(first + head, 1), part]
            odds = jnp.where(live_ref[1:2, part] > 0.0, jnp.exp(other - own), 0.0)
            share = jnp.where(live_ref[0:1, part] > 0.0, 1.0 / (1.0 + odds), 0.0)
            slope = lax.dot_general(
                value_ref[...], grad_ref[part, :], NT, preferred_element_type=F32
            )
            slope = pick_entry(slope, entry)
            low = (weight_ref[0, :, part] * share).astype(BF16).astype(F32)
            slope_ref[0, :, part] = slope
            share_ref[pl.ds(head, 1), part] = share
            dot_ref[pl.ds(head, 1), part] = jnp.sum(low * slope, axis=0, keepdims=True)

    return pl.pallas_call(
        body,
        grid=(here,),
        out_shape=(
            jax.ShapeDtypeStruct((here, LANES, rows), F32),
            jax.ShapeDtypeStruct((here, rows), F32),
            jax.ShapeDtypeStruct((here, rows), F32),
        ),
        in_specs=[
            pl.BlockSpec(memory_space=pltpu.SMEM),
            pl.BlockSpec((1, LANES, rows), lambda h: (first + h, 0, 0)),
            pl.BlockSpec((heads, rows), lambda h: (0, 0)),
            pl.BlockSpec((devices, heads, rows), lambda h: (0, 0, 0)),
            pl.BlockSpec((2, rows), lambda h: (0, 0)),
            pl.BlockSpec((rows, HEAD), lambda h: (0, h)),
            pl.BlockSpec((value_rows, HEAD), lambda h: (0, first + h)),
            pl.BlockSpec((1, rows), lambda h: (0, 0)),
        ],
        out_specs=(
            pl.BlockSpec((1, LANES, rows), lambda h: (h, 0, 0)),
            pl.BlockSpec((here, rows), lambda h: (0, 0)),
            pl.BlockSpec((here, rows), lambda h: (0, 0)),
        ),
        scratch_shapes=[pltpu.VMEM((heads, rows), F32)],
        name="weight_grads",
        **vmem_params(2 * rows * value_rows * here * HEAD, 10 * here * LANES * rows),
    )(partner, weights, lse, all_lse, live_lanes, grad_rows, values, entry_lanes)


def score_grads(chunk, weights, share, slope, dots, all_dots, partner, keys, entry_lanes):
    _, _, rows = weights.shape
    here = slope.shape[0]
    first = chunk * here
    key_rows = keys.shape[0]
    slots = rows // BLOCK
    devices = all_dots.shape[0]
    scale = 1.0 / math.sqrt(HEAD)

    def body(
        partner_ref,
        weight_ref,
        share_ref,
        slope_ref,
        dot_ref,
        all_ref,
        key_ref,
        entry_ref,
        low_ref,
        query_ref,
        other_ref,
    ):
        head = pl.program_id(0)

        @pl.when(head == 0)
        def _():
            partner_lanes(partner_ref, all_ref, other_ref, slots)

        for part in lane_parts(rows):
            entry = entry_ref[:, part]
            dot = dot_ref[pl.ds(head, 1), part] + other_ref[pl.ds(head, 1), part]
            joint = weight_ref[0, :, part] * share_ref[pl.ds(head, 1), part]
            low = joint * (slope_ref[0, :, part] - dot)
            low_ref[0, :, part] = low.astype(BF16)
            wide = spread_entry(low, entry, key_rows // LANES)
            query = lax.dot_general(wide, key_ref[...], TN, preferred_element_type=F32)
            query_ref[part, :] = (query * scale).astype(BF16)

    return pl.pallas_call(
        body,
        grid=(here,),
        out_shape=(
            jax.ShapeDtypeStruct((here, LANES, rows), BF16),
            jax.ShapeDtypeStruct((rows, here * HEAD), BF16),
        ),
        in_specs=[
            pl.BlockSpec(memory_space=pltpu.SMEM),
            pl.BlockSpec((1, LANES, rows), lambda h: (first + h, 0, 0)),
            pl.BlockSpec((here, rows), lambda h: (0, 0)),
            pl.BlockSpec((1, LANES, rows), lambda h: (h, 0, 0)),
            pl.BlockSpec((here, rows), lambda h: (0, 0)),
            pl.BlockSpec((devices, here, rows), lambda h: (0, 0, 0)),
            pl.BlockSpec((key_rows, HEAD), lambda h: (0, first + h)),
            pl.BlockSpec((1, rows), lambda h: (0, 0)),
        ],
        out_specs=(
            pl.BlockSpec((1, LANES, rows), lambda h: (h, 0, 0)),
            pl.BlockSpec((rows, HEAD), lambda h: (0, h)),
        ),
        scratch_shapes=[pltpu.VMEM((here, rows), F32)],
        name="score_grads",
        **vmem_params(2 * rows * key_rows * here * HEAD, 12 * here * LANES * rows),
    )(partner, weights, share, slope, dots, all_dots, keys, entry_lanes)


def entry_grads(chunk, weights, share, low, query_rows, grad_rows, entry_lanes, entry_rows):
    _, _, rows = weights.shape
    here = low.shape[0]
    first = chunk * here
    scale = 1.0 / math.sqrt(HEAD)

    def body(weight_ref, share_ref, low_ref, query_ref, grad_ref, entry_ref, key_ref, value_ref):
        head = pl.program_id(0)
        key_sum = jnp.zeros((entry_rows, HEAD), F32)
        value_sum = jnp.zeros((entry_rows, HEAD), F32)
        for part in lane_parts(rows):
            entry = entry_ref[:, part]
            joint = weight_ref[0, :, part] * share_ref[pl.ds(head, 1), part]
            wide = spread_entry(joint, entry, entry_rows // LANES)
            value_sum += lax.dot_general(wide, grad_ref[part, :], NN, preferred_element_type=F32)
            wide = spread_entry(low_ref[0, :, part].astype(F32), entry, entry_rows // LANES)
            key_sum += lax.dot_general(wide, query_ref[part, :], NN, preferred_element_type=F32)
        key_ref[...] = (key_sum * scale).astype(BF16)
        value_ref[...] = value_sum.astype(BF16)

    return pl.pallas_call(
        body,
        grid=(here,),
        out_shape=(
            jax.ShapeDtypeStruct((entry_rows, here * HEAD), BF16),
            jax.ShapeDtypeStruct((entry_rows, here * HEAD), BF16),
        ),
        in_specs=[
            pl.BlockSpec((1, LANES, rows), lambda h: (first + h, 0, 0)),
            pl.BlockSpec((here, rows), lambda h: (0, 0)),
            pl.BlockSpec((1, LANES, rows), lambda h: (h, 0, 0)),
            pl.BlockSpec((rows, HEAD), lambda h: (0, first + h)),
            pl.BlockSpec((rows, HEAD), lambda h: (0, h)),
            pl.BlockSpec((1, rows), lambda h: (0, 0)),
        ],
        out_specs=(
            pl.BlockSpec((entry_rows, HEAD), lambda h: (0, h)),
            pl.BlockSpec((entry_rows, HEAD), lambda h: (0, h)),
        ),
        name="entry_grads",
        **vmem_params(4 * rows * entry_rows * here * HEAD, 8 * here * LANES * rows),
    )(weights, share, low, query_rows, grad_rows, entry_lanes)


def swap(value, axis, bits):
    size = lax.axis_size(axis)
    return lax.ppermute(value, axis, [(i, i ^ bits) for i in range(size)])


def cube_gather(value, axis):
    value, bits = value[None], 1
    while bits < lax.axis_size(axis):
        value = jnp.concatenate([value, swap(value, axis, bits)], axis=0)
        bits *= 2
    return value


def rank_slots(owners):
    slot_total = owners.shape[-1]
    earlier_mask = jnp.arange(slot_total)[None, :] < jnp.arange(slot_total)[:, None]
    same_owner = owners[..., :, None] == owners[..., None, :]
    return jnp.sum(same_owner & earlier_mask, axis=-1)


def owner_tables(all_lists, counts_all, my_index, entries_here, slot_cap):
    n_seq, places = all_lists.shape
    owners = all_lists // entries_here
    ranks = rank_slots(owners)
    chosen = (owners == my_index)[:, None, :] & (
        ranks[:, None, :] == jnp.arange(slot_cap)[None, :, None]
    )
    place = jnp.arange(places)

    def look(table):
        return jnp.sum(jnp.where(chosen, table[:, None, :], 0), axis=2).reshape(-1)

    def other(table):
        return table.reshape(n_seq, -1, NEIGH)[:, :, ::-1].reshape(n_seq, places)

    entry = look(all_lists % entries_here)
    device = look(other(owners) ^ my_index)
    there = look(other(ranks) + slot_cap * jnp.arange(n_seq)[:, None])
    per_place = jnp.repeat(counts_all.reshape(n_seq, -1), NEIGH, axis=1)
    own_live = look((place % NEIGH < per_place).astype(jnp.int32))
    other_live = look((NEIGH - 1 - place % NEIGH < per_place).astype(jnp.int32))
    live = jnp.stack([own_live, other_live]).astype(F32)
    lanes = functools.partial(jnp.repeat, repeats=BLOCK, axis=-1)
    return (
        lanes(entry[None]).astype(jnp.int32),
        jnp.stack([device, there]).astype(jnp.int32),
        lanes(live),
    )


def on_device(out_grad, out_weight, queries, keys, values, retrieval, counts):
    n_seq, n_mp = lax.axis_size("seq"), lax.axis_size("mp")
    my_index, my_mp = lax.axis_index("seq"), lax.axis_index("mp")
    tok_rows, head_cols = queries.shape
    entries_here, nbr_rows, _ = keys.shape
    blocks_here = tok_rows // BLOCK
    places = blocks_here * NEIGH
    slot_cap = (places + n_seq - 1) // n_seq
    rows = n_seq * slot_cap * BLOCK
    feats = out_grad.shape[1]
    chunk_cols = head_cols // HEAD_CHUNKS
    lists_flat = retrieval.reshape(-1).astype(jnp.int32)
    index_arr = my_index.astype(jnp.int32).reshape(1)
    key_rows = keys.reshape(entries_here * nbr_rows, head_cols)
    value_rows = values.reshape(entries_here * nbr_rows, head_cols)

    def exchange(slot_rows):
        cols = slot_rows.shape[-1]
        return lax.all_to_all(
            slot_rows.reshape(n_seq, slot_cap * BLOCK, cols), "seq", 0, 0, tiled=True
        ).reshape(rows, cols)

    def to_owners(token_rows):
        return exchange(
            place_rows(token_rows, lists_flat, index_arr, n_seq, slot_cap, entries_here)
        )

    query_slots = to_owners(queries)
    counts_all = lax.all_gather(counts, "seq", axis=0, tiled=True)
    entry_lanes, partner, live_lanes = owner_tables(
        retrieval.reshape(n_seq, places), counts_all, my_index, entries_here, slot_cap
    )

    def product(part, source, at):
        weight = lax.dynamic_slice_in_dim(
            out_weight, source * feats + at, part.shape[1], axis=1
        )
        return lax.dot_general(part, weight, NT, preferred_element_type=F32)

    steps = 2
    width = feats // steps
    arrived = []
    for bits in range(2, n_mp, 2):
        for step in range(steps):
            piece = swap(out_grad[:, step * width : (step + 1) * width], "mp", bits)
            arrived.append((piece, my_mp ^ bits, step * width))
            arrived.append((swap(piece, "mp", 1), my_mp ^ bits ^ 1, step * width))
    grad_sum = product(out_grad, my_mp, 0) + product(swap(out_grad, "mp", 1), my_mp ^ 1, 0)
    for piece, source, at in arrived:
        grad_sum = grad_sum + product(piece, source, at)
    grad_out = grad_sum.astype(BF16)

    weights, lse = local_softmax(query_slots, key_rows, entry_lanes)
    all_lse = cube_gather(lse, "seq")

    query_parts, key_parts, value_parts = [], [], []
    for chunk in range(HEAD_CHUNKS):
        grad_slots = to_owners(grad_out[:, chunk * chunk_cols : (chunk + 1) * chunk_cols])
        slope, share, dots = weight_grads(
            chunk, weights, lse, all_lse, partner, live_lanes, grad_slots, value_rows, entry_lanes
        )
        low, query_terms = score_grads(
            chunk,
            weights,
            share,
            slope,
            dots,
            cube_gather(dots, "seq"),
            partner,
            key_rows,
            entry_lanes,
        )
        back = exchange(query_terms).reshape(-1, BLOCK, chunk_cols)
        query_parts.append(
            join_places(
                back, lists_flat, index_arr, n_seq, slot_cap, entries_here, blocks_here
            )
        )
        key_part, value_part = entry_grads(
            chunk, weights, share, low, query_slots, grad_slots, entry_lanes, key_rows.shape[0]
        )
        key_parts.append(key_part)
        value_parts.append(value_part)
    query_grad = jnp.concatenate(query_parts, axis=1)
    key_grad = jnp.concatenate(key_parts, axis=1).reshape(keys.shape)
    value_grad = jnp.concatenate(value_parts, axis=1).reshape(values.shape)
    return (query_grad, key_grad, value_grad)


def solution(mesh):
    return jax.shard_map(
        on_device,
        mesh=mesh,
        in_specs=(
            P("seq", "mp"),
            P("mp", None),
            P("seq", "mp"),
            P("seq", None, "mp"),
            P("seq", None, "mp"),
            P(),
            P("seq"),
        ),
        out_specs=(P("seq", "mp"), P("seq", None, "mp"), P("seq", None, "mp")),
        check_vma=False,
    )
```

```python
import functools
import math

import jax
import jax.numpy as jnp
from jax import lax
from jax.experimental import pallas as pl
from jax.experimental.pallas import tpu as pltpu
from jax.sharding import PartitionSpec as P

HEAD = 128
BLOCK = 64
NEIGH = 2
LANES = 128
HEAD_CHUNKS = 1
F32 = jnp.float32
BF16 = jnp.bfloat16


def vmem_params(flops=0, moved=0, mib=48):
    return dict(
        compiler_params=pltpu.CompilerParams(vmem_limit_bytes=mib * 1024 * 1024),
        cost_estimate=pl.CostEstimate(flops=flops, bytes_accessed=moved, transcendentals=0),
    )


def slot_of_place(lists_ref, base, place, entries_here, slot_cap):
    owner = lists_ref[base + place] // entries_here
    rank = 0
    for earlier in range(place):
        rank = rank + jnp.where(lists_ref[base + earlier] // entries_here == owner, 1, 0)
    return owner * slot_cap + rank


def place_copies(lists_ref, base, rows_ref, out_refs, zero_ref, sems, places, entries_here, slot_cap):
    slots = out_refs[0].shape[0]
    width = out_refs[0].shape[2]
    if slots > places:
        zero_ref[...] = jnp.zeros_like(zero_ref)
        for chunk, out_ref in enumerate(out_refs):
            blanks = [
                pltpu.make_async_copy(zero_ref, out_ref.at[slot], sems.at[chunk, slot])
                for slot in range(slots)
            ]
            for blank in blanks:
                blank.start()
            for blank in blanks:
                blank.wait()
    slot_list = [
        slot_of_place(lists_ref, base, place, entries_here, slot_cap) for place in range(places)
    ]
    copies = []
    for chunk, out_ref in enumerate(out_refs):
        for place, slot in enumerate(slot_list):
            start = place // NEIGH * BLOCK
            copies.append(
                pltpu.make_async_copy(
                    rows_ref.at[pl.ds(start, BLOCK), pl.ds(chunk * width, width)],
                    out_ref.at[slot],
                    sems.at[chunk, place],
                )
            )
            copies[-1].start()
    for copy in copies:
        copy.wait()


def place_rows(rows, lists_flat, my_index, n_seq, slot_cap, entries_here):
    tok_rows, cols = rows.shape
    places = tok_rows // BLOCK * NEIGH
    slots = n_seq * slot_cap

    def body(lists_ref, index_ref, rows_ref, out_ref, zero_ref, sems):
        place_copies(
            lists_ref,
            index_ref[0] * places,
            rows_ref,
            [out_ref],
            zero_ref,
            sems,
            places,
            entries_here,
            slot_cap,
        )

    return pl.pallas_call(
        body,
        out_shape=jax.ShapeDtypeStruct((slots, BLOCK, cols), rows.dtype),
        in_specs=[
            pl.BlockSpec(memory_space=pltpu.SMEM),
            pl.BlockSpec(memory_space=pltpu.SMEM),
            pl.BlockSpec(memory_space=pltpu.VMEM),
        ],
        out_specs=pl.BlockSpec(memory_space=pl.ANY),
        scratch_shapes=[
            pltpu.VMEM((BLOCK, cols), rows.dtype),
            pltpu.SemaphoreType.DMA((1, max(slots, places))),
        ],
        name="place_rows",
        **vmem_params(moved=2 * slots * BLOCK * cols * 2, mib=60),
    )(lists_flat, my_index, rows)


def add_product(total, parts, weight, sources, placing=None):
    tok_rows, width = parts[0].shape
    feats = weight.shape[1] // lax.axis_size("mp")
    unit = math.gcd(width, feats)
    cuts = range(width // unit)
    first_units = [source * (feats // unit) + at // unit for source, at in sources]
    cols = weight.shape[0]
    step_cols = min(256, cols)
    steps = cols // step_cols
    places = tok_rows // BLOCK * NEIGH
    before = [] if total is None else [total]
    if placing is None:
        chunks = 1
    else:
        lists_flat, my_index, n_seq, slot_cap, entries_here, chunks = placing
        slots = n_seq * slot_cap

    def body(source_ref, *refs):
        refs = list(refs)
        place_refs = [refs.pop(0) for _ in range(2)] if placing is not None else None
        before_ref = refs.pop(0) if before else None
        part_refs = [refs.pop(0) for _ in parts]
        weight_refs = [[refs.pop(0) for _ in cuts] for _ in parts]
        out_refs = [refs.pop(0) for _ in range(chunks)]
        step = pl.program_id(0)
        result = before_ref[...] if before else 0.0
        for part_ref, weight_cuts in zip(part_refs, weight_refs):
            for cut, weight_ref in zip(cuts, weight_cuts):
                result = result + lax.dot_general(
                    part_ref[:, cut * unit : (cut + 1) * unit],
                    weight_ref[...],
                    NT,
                    preferred_element_type=F32,
                )
        if placing is None:
            out_refs[0][...] = result
            return
        low_ref, zero_ref, sems = refs
        low_ref[:, pl.ds(pl.multiple_of(step * step_cols, step_cols), step_cols)] = result.astype(
            BF16
        )

        @pl.when(step == steps - 1)
        def _():
            lists_ref, index_ref = place_refs
            place_copies(
                lists_ref,
                index_ref[0] * places,
                low_ref,
                out_refs,
                zero_ref,
                sems,
                places,
                entries_here,
                slot_cap,
            )

    block = pl.BlockSpec((tok_rows, step_cols), lambda k, s: (0, k))
    in_specs = [block] * len(before)
    in_specs += [pl.BlockSpec((tok_rows, width), lambda k, s: (0, 0))] * len(parts)
    for number in range(len(parts)):
        for cut in cuts:
            in_specs.append(
                pl.BlockSpec((step_cols, unit), lambda k, s, n=number, c=cut: (k, s[n] + c))
            )
    if placing is None:
        out_shape, out_specs = [jax.ShapeDtypeStruct((tok_rows, cols), F32)], [block]
        scratch, extra = [], []
    else:
        chunk_cols = cols // chunks
        out_shape = [jax.ShapeDtypeStruct((slots, BLOCK, chunk_cols), BF16)] * chunks
        out_specs = [pl.BlockSpec(memory_space=pl.ANY)] * chunks
        scratch = [
            pltpu.VMEM((tok_rows, cols), BF16),
            pltpu.VMEM((BLOCK, chunk_cols), BF16),
            pltpu.SemaphoreType.DMA((chunks, max(slots, places))),
        ]
        extra = [lists_flat, my_index]
        in_specs = [pl.BlockSpec(memory_space=pltpu.SMEM)] * 2 + in_specs
    return pl.pallas_call(
        body,
        grid_spec=pltpu.PrefetchScalarGridSpec(
            num_scalar_prefetch=1,
            grid=(steps,),
            in_specs=in_specs,
            out_specs=out_specs,
            scratch_shapes=scratch,
        ),
        out_shape=out_shape,
        name="add_product",
        **vmem_params(moved=1, mib=60),
    )(
        jnp.stack(first_units).astype(jnp.int32),
        *extra,
        *before,
        *parts,
        *[weight] * (len(parts) * len(cuts)),
    )


def join_places(
    chunk, chunks, back, before, lists_flat, my_index, n_seq, slot_cap, entries_here, blocks_here
):
    slots, _, cols = back.shape
    places = blocks_here * NEIGH
    kept = [] if before is None else [before]

    def body(lists_ref, index_ref, back_ref, *refs):
        out_ref = refs[-1]
        base = index_ref[0] * places
        for block in range(blocks_here):
            total = 0.0
            for neighbour in range(NEIGH):
                slot = slot_of_place(
                    lists_ref, base, block * NEIGH + neighbour, entries_here, slot_cap
                )
                total = total + back_ref[slot].astype(F32)
            out_ref[block * BLOCK : (block + 1) * BLOCK, :] = total.astype(out_ref.dtype)

    return pl.pallas_call(
        body,
        grid=(1,),
        out_shape=jax.ShapeDtypeStruct((blocks_here * BLOCK, chunks * cols), back.dtype),
        in_specs=[
            pl.BlockSpec(memory_space=pltpu.SMEM),
            pl.BlockSpec(memory_space=pltpu.SMEM),
            pl.BlockSpec((slots, BLOCK, cols), lambda i: (0, 0, 0)),
        ]
        + [pl.BlockSpec(memory_space=pl.ANY)] * len(kept),
        out_specs=pl.BlockSpec((blocks_here * BLOCK, cols), lambda i: (0, chunk)),
        input_output_aliases={3: 0} if kept else {},
        name="join_places",
        **vmem_params(moved=3 * slots * BLOCK * cols),
    )(lists_flat, my_index, back, *kept)


def lane_parts(total):
    width = 256 if total % 256 == 0 else LANES
    return [slice(at, at + width) for at in range(0, total, width)]


def pick_entry(stacked, entry):
    entries = stacked.shape[0] // LANES
    chosen = stacked[:LANES]
    for number in range(1, entries):
        chosen = jnp.where(
            entry == number, stacked[number * LANES : (number + 1) * LANES], chosen
        )
    return chosen


def spread_entry(chosen, entry, entries):
    return jnp.concatenate(
        [jnp.where(entry == number, chosen, 0.0) for number in range(entries)], axis=0
    ).astype(BF16)


NT = (((1,), (1,)), ((), ()))
NN = (((1,), (0,)), ((), ()))
TN = (((0,), (0,)), ((), ()))


def local_softmax(query_rows, keys, entry_lanes):
    rows, cols = query_rows.shape
    heads = cols // HEAD
    key_rows = keys.shape[0]
    scale = 1.0 / math.sqrt(HEAD)

    def body(query_ref, key_ref, entry_ref, weight_ref, lse_ref):
        head = pl.program_id(0)
        for part in lane_parts(rows):
            entry = entry_ref[:, part]
            scores = lax.dot_general(
                key_ref[...], query_ref[part, :], NT, preferred_element_type=F32
            )
            scores = pick_entry(scores, entry) * scale
            top = jnp.max(scores, axis=0, keepdims=True)
            raised = jnp.exp(scores - top)
            total = jnp.sum(raised, axis=0, keepdims=True)
            weight_ref[0, :, part] = raised / total
            lse_ref[pl.ds(head, 1), part] = top + jnp.log(total)

    return pl.pallas_call(
        body,
        grid=(heads,),
        out_shape=(
            jax.ShapeDtypeStruct((heads, LANES, rows), F32),
            jax.ShapeDtypeStruct((heads, rows), F32),
        ),
        in_specs=[
            pl.BlockSpec((rows, HEAD), lambda h: (0, h)),
            pl.BlockSpec((key_rows, HEAD), lambda h: (0, h)),
            pl.BlockSpec((1, rows), lambda h: (0, 0)),
        ],
        out_specs=(
            pl.BlockSpec((1, LANES, rows), lambda h: (h, 0, 0)),
            pl.BlockSpec((heads, rows), lambda h: (0, 0)),
        ),
        name="local_softmax",
        **vmem_params(moved=1, mib=60),
    )(query_rows, keys, entry_lanes)


def partner_lanes(partner_ref, all_ref, out_ref, slots):
    heads = out_ref.shape[0]
    lane = lax.broadcasted_iota(jnp.int32, (heads, LANES), 1)
    for group in range(slots // 2):
        halves = []
        for half in range(2):
            slot = group * 2 + half
            device, there = partner_ref[0, slot], partner_ref[1, slot]
            start = pl.multiple_of(there // 2 * LANES, LANES)
            tile = all_ref[device, :, pl.ds(start, LANES)]
            turned = pltpu.roll(tile, BLOCK, 1)
            halves.append(jnp.where(there % 2 == half, tile, turned))
        out_ref[:, group * LANES : (group + 1) * LANES] = jnp.where(
            lane < BLOCK, halves[0], halves[1]
        )


def live_lanes(partner_ref, all_ref, out_ref, slots, rows):
    lane = lax.broadcasted_iota(jnp.int32, (1, LANES), 1)
    for group in range(slots // 2):
        own, other = [], []
        for half in range(2):
            slot = group * 2 + half
            reader, place = partner_ref[2, slot], partner_ref[3, slot]
            counts = all_ref[reader, 0:1, rows:]
            count = jnp.sum(
                jnp.where(lane == place // NEIGH, counts, 0.0), axis=1, keepdims=True
            )
            at = (place % NEIGH).astype(F32)
            filled = partner_ref[4, slot] > 0
            own.append(jnp.where((at < count) & filled, 1.0, 0.0))
            other.append(jnp.where(NEIGH - 1 - at < count, 1.0, 0.0))
        part = slice(group * LANES, (group + 1) * LANES)
        out_ref[0:1, part] = jnp.where(lane < BLOCK, own[0], own[1])
        out_ref[1:2, part] = jnp.where(lane < BLOCK, other[0], other[1])


def weight_grads(n_seq, weights, lse, grad_rows, values, entry_lanes, count_lanes):
    heads, _, rows = weights.shape
    value_rows = values.shape[0]

    def body(
        weight_ref, lse_ref, grad_ref, value_ref, entry_ref, count_ref, slope_ref, all_ref, told_ref
    ):
        head = pl.program_id(0)

        @pl.when(head == 0)
        def _():
            told_ref[:heads, :rows] = lse_ref[...]
            told_ref[:, rows:] = jnp.broadcast_to(count_ref[...], (2 * heads, LANES))

        for part in lane_parts(rows):
            slope = lax.dot_general(
                value_ref[...], grad_ref[part, :], NT, preferred_element_type=F32
            )
            slope = pick_entry(slope, entry_ref[:, part])
            slope_ref[0, :, part] = slope
            told_ref[pl.ds(heads + head, 1), part] = jnp.sum(
                weight_ref[0, :, part] * slope, axis=0, keepdims=True
            )

        @pl.when(head == heads - 1)
        def _():
            for device in range(n_seq):
                all_ref[device] = told_ref[...]

    return pl.pallas_call(
        body,
        grid=(heads,),
        out_shape=(
            jax.ShapeDtypeStruct((heads, LANES, rows), F32),
            jax.ShapeDtypeStruct((n_seq, 2 * heads, rows + LANES), F32),
        ),
        in_specs=[
            pl.BlockSpec((1, LANES, rows), lambda h: (h, 0, 0)),
            pl.BlockSpec((heads, rows), lambda h: (0, 0)),
            pl.BlockSpec((rows, HEAD), lambda h: (0, h)),
            pl.BlockSpec((value_rows, HEAD), lambda h: (0, h)),
            pl.BlockSpec((1, rows), lambda h: (0, 0)),
            pl.BlockSpec((1, LANES), lambda h: (0, 0)),
        ],
        out_specs=(
            pl.BlockSpec((1, LANES, rows), lambda h: (h, 0, 0)),
            pl.BlockSpec((n_seq, 2 * heads, rows + LANES), lambda h: (0, 0, 0)),
        ),
        scratch_shapes=[pltpu.VMEM((2 * heads, rows + LANES), F32)],
        name="weight_grads",
        **vmem_params(moved=1, mib=60),
    )(weights, lse, grad_rows, values, entry_lanes, count_lanes)


def score_grads(weights, slope, all_told, my_index, partner, keys, entry_lanes):
    here, _, rows = weights.shape
    key_rows = keys.shape[0]
    slots = rows // BLOCK
    scale = 1.0 / math.sqrt(HEAD)

    def body(
        partner_ref,
        index_ref,
        weight_ref,
        slope_ref,
        all_ref,
        key_ref,
        entry_ref,
        share_ref,
        low_ref,
        query_ref,
        told_ref,
        other_ref,
        live_ref,
    ):
        head = pl.program_id(0)

        @pl.when(head == 0)
        def _():
            told_ref[...] = all_ref[index_ref[0], :, :rows]
            partner_lanes(partner_ref, all_ref, other_ref, slots)
            live_lanes(partner_ref, all_ref, live_ref, slots, rows)

        for part in lane_parts(rows):
            entry = entry_ref[:, part]
            apart = other_ref[pl.ds(head, 1), part] - told_ref[pl.ds(head, 1), part]
            odds = jnp.where(live_ref[1:2, part] > 0.0, jnp.exp(apart), 0.0)
            share = jnp.where(live_ref[0:1, part] > 0.0, 1.0 / (1.0 + odds), 0.0)
            rest = jnp.where(live_ref[1:2, part] > 0.0, 1.0 / (1.0 + jnp.exp(-apart)), 0.0)
            dot = (
                share * told_ref[pl.ds(here + head, 1), part]
                + rest * other_ref[pl.ds(here + head, 1), part]
            )
            share_ref[pl.ds(head, 1), part] = share
            joint = weight_ref[0, :, part] * share
            low = joint * (slope_ref[0, :, part] - dot)
            low_ref[0, :, part] = low.astype(BF16)
            wide = spread_entry(low, entry, key_rows // LANES)
            query = lax.dot_general(wide, key_ref[...], TN, preferred_element_type=F32)
            query_ref[part, :] = (query * scale).astype(BF16)

    return pl.pallas_call(
        body,
        grid=(here,),
        out_shape=(
            jax.ShapeDtypeStruct((here, rows), F32),
            jax.ShapeDtypeStruct((here, LANES, rows), BF16),
            jax.ShapeDtypeStruct((rows, here * HEAD), BF16),
        ),
        in_specs=[
            pl.BlockSpec(memory_space=pltpu.SMEM),
            pl.BlockSpec(memory_space=pltpu.SMEM),
            pl.BlockSpec((1, LANES, rows), lambda h: (h, 0, 0)),
            pl.BlockSpec((1, LANES, rows), lambda h: (h, 0, 0)),
            pl.BlockSpec(all_told.shape, lambda h: (0, 0, 0)),
            pl.BlockSpec((key_rows, HEAD), lambda h: (0, h)),
            pl.BlockSpec((1, rows), lambda h: (0, 0)),
        ],
        out_specs=(
            pl.BlockSpec((here, rows), lambda h: (0, 0)),
            pl.BlockSpec((1, LANES, rows), lambda h: (h, 0, 0)),
            pl.BlockSpec((rows, HEAD), lambda h: (0, h)),
        ),
        scratch_shapes=[
            pltpu.VMEM((2 * here, rows), F32),
            pltpu.VMEM((2 * here, rows), F32),
            pltpu.VMEM((2, rows), F32),
        ],
        name="score_grads",
        **vmem_params(moved=1, mib=60),
    )(partner, my_index, weights, slope, all_told, keys, entry_lanes)


def entry_grads(chunk, weights, share, low, query_rows, grad_rows, entry_lanes, entry_rows):
    _, _, rows = weights.shape
    here = low.shape[0]
    first = chunk * here
    scale = 1.0 / math.sqrt(HEAD)

    def body(weight_ref, share_ref, low_ref, query_ref, grad_ref, entry_ref, key_ref, value_ref):
        head = pl.program_id(0)
        key_sum = jnp.zeros((entry_rows, HEAD), F32)
        value_sum = jnp.zeros((entry_rows, HEAD), F32)
        for part in lane_parts(rows):
            entry = entry_ref[:, part]
            joint = weight_ref[0, :, part] * share_ref[pl.ds(head, 1), part]
            wide = spread_entry(joint, entry, entry_rows // LANES)
            value_sum += lax.dot_general(wide, grad_ref[part, :], NN, preferred_element_type=F32)
            wide = spread_entry(low_ref[0, :, part].astype(F32), entry, entry_rows // LANES)
            key_sum += lax.dot_general(wide, query_ref[part, :], NN, preferred_element_type=F32)
        key_ref[...] = (key_sum * scale).astype(BF16)
        value_ref[...] = value_sum.astype(BF16)

    return pl.pallas_call(
        body,
        grid=(here,),
        out_shape=(
            jax.ShapeDtypeStruct((entry_rows, here * HEAD), BF16),
            jax.ShapeDtypeStruct((entry_rows, here * HEAD), BF16),
        ),
        in_specs=[
            pl.BlockSpec((1, LANES, rows), lambda h: (first + h, 0, 0)),
            pl.BlockSpec((here, rows), lambda h: (0, 0)),
            pl.BlockSpec((1, LANES, rows), lambda h: (h, 0, 0)),
            pl.BlockSpec((rows, HEAD), lambda h: (0, first + h)),
            pl.BlockSpec((rows, HEAD), lambda h: (0, h)),
            pl.BlockSpec((1, rows), lambda h: (0, 0)),
        ],
        out_specs=(
            pl.BlockSpec((entry_rows, HEAD), lambda h: (0, h)),
            pl.BlockSpec((entry_rows, HEAD), lambda h: (0, h)),
        ),
        name="entry_grads",
        **vmem_params(moved=1, mib=60),
    )(weights, share, low, query_rows, grad_rows, entry_lanes)


def swap(value, axis, bits):
    size = lax.axis_size(axis)
    return lax.ppermute(value, axis, [(i, i ^ bits) for i in range(size)])


def rank_slots(owners):
    slot_total = owners.shape[-1]
    earlier_mask = jnp.arange(slot_total)[None, :] < jnp.arange(slot_total)[:, None]
    same_owner = owners[..., :, None] == owners[..., None, :]
    return jnp.sum(same_owner & earlier_mask, axis=-1)


def owner_tables(all_lists, my_index, entries_here, slot_cap):
    n_seq, places = all_lists.shape
    owners = all_lists // entries_here
    ranks = rank_slots(owners)
    chosen = (owners == my_index)[:, None, :] & (
        ranks[:, None, :] == jnp.arange(slot_cap)[None, :, None]
    )

    def look(table):
        return jnp.sum(jnp.where(chosen, table[:, None, :], 0), axis=2).reshape(-1)

    def other(table):
        return table.reshape(n_seq, -1, NEIGH)[:, :, ::-1].reshape(n_seq, places)

    reader = jnp.arange(n_seq)[:, None]
    partner = [
        look(other(owners)),
        look(other(ranks) + slot_cap * reader),
        look(reader + jnp.zeros_like(owners)),
        look(jnp.arange(places) + jnp.zeros_like(owners)),
        look(jnp.ones_like(owners)),
    ]
    entry = look(all_lists % entries_here)
    return (
        jnp.repeat(entry[None], BLOCK, axis=1).astype(jnp.int32),
        jnp.stack(partner).astype(jnp.int32),
    )


def on_device(out_grad, out_weight, queries, keys, values, retrieval, counts):
    n_seq, n_mp = lax.axis_size("seq"), lax.axis_size("mp")
    my_index, my_mp = lax.axis_index("seq"), lax.axis_index("mp")
    tok_rows, head_cols = queries.shape
    entries_here, nbr_rows, _ = keys.shape
    blocks_here = tok_rows // BLOCK
    places = blocks_here * NEIGH
    slot_cap = (places + n_seq - 1) // n_seq
    rows = n_seq * slot_cap * BLOCK
    feats = out_grad.shape[1]
    lists_flat = retrieval.reshape(-1).astype(jnp.int32)
    index_arr = my_index.astype(jnp.int32).reshape(1)
    key_rows = keys.reshape(entries_here * nbr_rows, head_cols)
    value_rows = values.reshape(entries_here * nbr_rows, head_cols)

    def exchange(slot_rows):
        cols = slot_rows.shape[-1]
        return lax.all_to_all(
            slot_rows.reshape(n_seq, slot_cap * BLOCK, cols), "seq", 0, 0, tiled=True
        ).reshape(rows, cols)

    far_bits = list(range(2, n_mp, 2))
    cut = feats * 3 // 4
    tie = lax.optimization_barrier

    def sources(at):
        return [(my_mp ^ bits ^ side, at) for bits in far_bits for side in (0, 1)]

    def both_cores(pieces):
        return [x for piece in pieces for x in (piece, swap(piece, "mp", 1))]

    near = swap(out_grad, "mp", 1)
    first = [swap(out_grad[:, :cut], "mp", bits) for bits in far_bits]
    near, outgoing = tie((near, queries))
    query_places = place_rows(outgoing, lists_flat, index_arr, n_seq, slot_cap, entries_here)
    query_slots = exchange(query_places)
    entry_lanes, partner = owner_tables(
        retrieval.reshape(n_seq, places), my_index, entries_here, slot_cap
    )

    placing = (lists_flat, index_arr, n_seq, slot_cap, entries_here, HEAD_CHUNKS)
    (grad_sum,) = add_product(None, [out_grad, near], out_weight, [(my_mp, 0), (my_mp ^ 1, 0)])
    second, first, grad_sum = tie((out_grad[:, cut:], first, grad_sum))
    second = [swap(second, "mp", bits) for bits in far_bits]
    (grad_sum,) = add_product(grad_sum, both_cores(first), out_weight, sources(0))
    second, grad_sum = tie((second, grad_sum))
    grad_sum = add_product(grad_sum, both_cores(second), out_weight, sources(cut), placing)
    grad_places = grad_sum

    count_lanes = jnp.pad(counts.astype(F32), (0, LANES - blocks_here))[None]
    weights, lse = local_softmax(query_slots, key_rows, entry_lanes)

    grad_slots = exchange(grad_places[0])
    slope, told = weight_grads(
        n_seq, weights, lse, grad_slots, value_rows, entry_lanes, count_lanes
    )
    all_told = lax.all_to_all(told, "seq", 0, 0, tiled=True)
    share, low, query_terms = score_grads(
        weights, slope, all_told, index_arr, partner, key_rows, entry_lanes
    )
    back = exchange(query_terms).reshape(-1, BLOCK, head_cols)
    query_grad = join_places(
        0, 1, back, None, lists_flat, index_arr, n_seq, slot_cap, entries_here, blocks_here
    )
    key_grad, value_grad = entry_grads(
        0, weights, share, low, query_slots, grad_slots, entry_lanes, key_rows.shape[0]
    )
    key_grad = key_grad.reshape(keys.shape)
    value_grad = value_grad.reshape(values.shape)
    return (query_grad, key_grad, value_grad)


def solution(mesh):
    return jax.shard_map(
        on_device,
        mesh=mesh,
        in_specs=(
            P("seq", "mp"),
            P("mp", None),
            P("seq", "mp"),
            P("seq", None, "mp"),
            P("seq", None, "mp"),
            P(),
            P("seq"),
        ),
        out_specs=(P("seq", "mp"), P("seq", None, "mp"), P("seq", None, "mp")),
        check_vma=False,
    )
```

```python
import functools
import math

import jax
import jax.numpy as jnp
from jax import lax
from jax.experimental import pallas as pl
from jax.experimental.pallas import tpu as pltpu
from jax.sharding import PartitionSpec as P

HEAD = 128
BLOCK = 64
NEIGH = 2
LANES = 128
HEAD_CHUNKS = 1
STEPS = 2
F32 = jnp.float32
BF16 = jnp.bfloat16


def vmem_params(flops=0, moved=0, mib=48):
    return dict(
        compiler_params=pltpu.CompilerParams(vmem_limit_bytes=mib * 1024 * 1024),
        cost_estimate=pl.CostEstimate(flops=flops, bytes_accessed=moved, transcendentals=0),
    )


def slot_of_place(lists_ref, base, place, entries_here, slot_cap):
    owner = lists_ref[base + place // NEIGH, place % NEIGH] // entries_here
    rank = 0
    for earlier in range(place):
        named = lists_ref[base + earlier // NEIGH, earlier % NEIGH]
        rank = rank + jnp.where(named // entries_here == owner, 1, 0)
    return owner * slot_cap + rank


def place_copies(lists_ref, base, rows_ref, out_refs, zero_ref, sems, places, entries_here, slot_cap):
    slots = out_refs[0].shape[0]
    width = out_refs[0].shape[2]
    if slots > places:
        zero_ref[...] = jnp.zeros_like(zero_ref)
        for chunk, out_ref in enumerate(out_refs):
            blanks = [
                pltpu.make_async_copy(zero_ref, out_ref.at[slot], sems.at[chunk, slot])
                for slot in range(slots)
            ]
            for blank in blanks:
                blank.start()
            for blank in blanks:
                blank.wait()
    slot_list = [
        slot_of_place(lists_ref, base, place, entries_here, slot_cap) for place in range(places)
    ]
    copies = []
    for chunk, out_ref in enumerate(out_refs):
        for place, slot in enumerate(slot_list):
            start = place // NEIGH * BLOCK
            copies.append(
                pltpu.make_async_copy(
                    rows_ref.at[pl.ds(start, BLOCK), pl.ds(chunk * width, width)],
                    out_ref.at[slot],
                    sems.at[chunk, place],
                )
            )
            copies[-1].start()
    for copy in copies:
        copy.wait()


def place_rows(rows, lists, my_index, n_seq, slot_cap, entries_here):
    tok_rows, cols = rows.shape
    places = tok_rows // BLOCK * NEIGH
    slots = n_seq * slot_cap

    def body(lists_ref, index_ref, rows_ref, out_ref, zero_ref, sems):
        place_copies(
            lists_ref,
            index_ref[0] * (places // NEIGH),
            rows_ref,
            [out_ref],
            zero_ref,
            sems,
            places,
            entries_here,
            slot_cap,
        )

    return pl.pallas_call(
        body,
        out_shape=jax.ShapeDtypeStruct((slots, BLOCK, cols), rows.dtype),
        in_specs=[
            pl.BlockSpec(memory_space=pltpu.SMEM),
            pl.BlockSpec(memory_space=pltpu.SMEM),
            pl.BlockSpec(memory_space=pltpu.VMEM),
        ],
        out_specs=pl.BlockSpec(memory_space=pl.ANY),
        scratch_shapes=[
            pltpu.VMEM((BLOCK, cols), rows.dtype),
            pltpu.SemaphoreType.DMA((1, max(slots, places))),
        ],
        name="place_rows",
        **vmem_params(moved=2 * slots * BLOCK * cols * 2, mib=60),
    )(lists, my_index, rows)


def add_product(total, parts, weight, sources, placing=None):
    tok_rows, width = parts[0].shape
    feats = weight.shape[1] // lax.axis_size("mp")
    unit = math.gcd(width, feats)
    cuts = range(width // unit)
    first_units = [source * (feats // unit) + at // unit for source, at in sources]
    cols = weight.shape[0]
    step_cols = cols // (2 * len(parts)) if len(parts) < 3 else min(256, cols)
    steps = cols // step_cols
    places = tok_rows // BLOCK * NEIGH
    before = [] if total is None else [total]
    if placing is None:
        chunks = 1
    else:
        lists, my_index, n_seq, slot_cap, entries_here, chunks = placing
        slots = n_seq * slot_cap

    def body(source_ref, *refs):
        refs = list(refs)
        place_refs = [refs.pop(0) for _ in range(2)] if placing is not None else None
        before_ref = refs.pop(0) if before else None
        part_refs = [refs.pop(0) for _ in parts]
        weight_refs = [[refs.pop(0) for _ in cuts] for _ in parts]
        out_refs = [refs.pop(0) for _ in range(chunks)]
        step = pl.program_id(0)
        result = before_ref[...] if before else 0.0
        for part_ref, weight_cuts in zip(part_refs, weight_refs):
            for cut, weight_ref in zip(cuts, weight_cuts):
                result = result + lax.dot_general(
                    part_ref[:, cut * unit : (cut + 1) * unit],
                    weight_ref[...],
                    NT,
                    preferred_element_type=F32,
                )
        if placing is None:
            out_refs[0][...] = result
            return
        low_ref, zero_ref, sems = refs
        low_ref[:, pl.ds(pl.multiple_of(step * step_cols, step_cols), step_cols)] = result.astype(
            BF16
        )

        @pl.when(step == steps - 1)
        def _():
            lists_ref, index_ref = place_refs
            place_copies(
                lists_ref,
                index_ref[0] * (places // NEIGH),
                low_ref,
                out_refs,
                zero_ref,
                sems,
                places,
                entries_here,
                slot_cap,
            )

    block = pl.BlockSpec((tok_rows, step_cols), lambda k, s: (0, k))
    in_specs = [block] * len(before)
    in_specs += [pl.BlockSpec((tok_rows, width), lambda k, s: (0, 0))] * len(parts)
    for number in range(len(parts)):
        for cut in cuts:
            in_specs.append(
                pl.BlockSpec((step_cols, unit), lambda k, s, n=number, c=cut: (k, s[n] + c))
            )
    if placing is None:
        out_shape, out_specs = [jax.ShapeDtypeStruct((tok_rows, cols), F32)], [block]
        scratch, extra = [], []
    else:
        chunk_cols = cols // chunks
        out_shape = [jax.ShapeDtypeStruct((slots, BLOCK, chunk_cols), BF16)] * chunks
        out_specs = [pl.BlockSpec(memory_space=pl.ANY)] * chunks
        scratch = [
            pltpu.VMEM((tok_rows, cols), BF16),
            pltpu.VMEM((BLOCK, chunk_cols), BF16),
            pltpu.SemaphoreType.DMA((chunks, max(slots, places))),
        ]
        extra = [lists, my_index]
        in_specs = [pl.BlockSpec(memory_space=pltpu.SMEM)] * 2 + in_specs
    return pl.pallas_call(
        body,
        grid_spec=pltpu.PrefetchScalarGridSpec(
            num_scalar_prefetch=1,
            grid=(steps,),
            in_specs=in_specs,
            out_specs=out_specs,
            scratch_shapes=scratch,
        ),
        out_shape=out_shape,
        name="add_product",
        **vmem_params(moved=1, mib=60),
    )(
        jnp.stack(first_units).astype(jnp.int32),
        *extra,
        *before,
        *parts,
        *[weight] * (len(parts) * len(cuts)),
    )


def join_places(
    chunk, chunks, back, before, lists, my_index, n_seq, slot_cap, entries_here, blocks_here
):
    slots, _, cols = back.shape
    places = blocks_here * NEIGH
    kept = [] if before is None else [before]

    def body(lists_ref, index_ref, back_ref, *refs):
        out_ref = refs[-1]
        base = index_ref[0] * (places // NEIGH)
        for block in range(blocks_here):
            total = 0.0
            for neighbour in range(NEIGH):
                slot = slot_of_place(
                    lists_ref, base, block * NEIGH + neighbour, entries_here, slot_cap
                )
                total = total + back_ref[slot].astype(F32)
            out_ref[block * BLOCK : (block + 1) * BLOCK, :] = total.astype(out_ref.dtype)

    return pl.pallas_call(
        body,
        grid=(1,),
        out_shape=jax.ShapeDtypeStruct((blocks_here * BLOCK, chunks * cols), back.dtype),
        in_specs=[
            pl.BlockSpec(memory_space=pltpu.SMEM),
            pl.BlockSpec(memory_space=pltpu.SMEM),
            pl.BlockSpec((slots, BLOCK, cols), lambda i: (0, 0, 0)),
        ]
        + [pl.BlockSpec(memory_space=pl.ANY)] * len(kept),
        out_specs=pl.BlockSpec((blocks_here * BLOCK, cols), lambda i: (0, chunk)),
        input_output_aliases={3: 0} if kept else {},
        name="join_places",
        **vmem_params(moved=3 * slots * BLOCK * cols),
    )(lists, my_index, back, *kept)


def lane_parts(total):
    width = 256 if total % 256 == 0 else LANES
    return [slice(at, at + width) for at in range(0, total, width)]


def pick_entry(stacked, entry):
    entries = stacked.shape[0] // LANES
    chosen = stacked[:LANES]
    for number in range(1, entries):
        chosen = jnp.where(
            entry == number, stacked[number * LANES : (number + 1) * LANES], chosen
        )
    return chosen


def spread_entry(chosen, entry, entries):
    return jnp.concatenate(
        [jnp.where(entry == number, chosen, 0.0) for number in range(entries)], axis=0
    ).astype(BF16)


NT = (((1,), (1,)), ((), ()))
NN = (((1,), (0,)), ((), ()))
TN = (((0,), (0,)), ((), ()))


def local_softmax(query_rows, keys, values, entry_lanes):
    rows, cols = query_rows.shape
    heads = cols // HEAD
    key_rows = keys.shape[0]
    scale = 1.0 / math.sqrt(HEAD)

    def body(query_ref, key_ref, value_ref, entry_ref, weight_ref, lse_ref, seen_ref, mean_ref):
        head = pl.program_id(0)
        for part in lane_parts(rows):
            entry = entry_ref[:, part]
            scores = lax.dot_general(
                key_ref[...], query_ref[part, :], NT, preferred_element_type=F32
            )
            scores = pick_entry(scores, entry) * scale
            top = jnp.max(scores, axis=0, keepdims=True)
            raised = jnp.exp(scores - top)
            total = jnp.sum(raised, axis=0, keepdims=True)
            weights = raised / total
            weight_ref[0, :, part] = weights
            lse_ref[pl.ds(head, 1), part] = top + jnp.log(total)
            wide = spread_entry(weights, entry, key_rows // LANES)
            seen_ref[part, :] = lax.dot_general(
                wide, value_ref[...], TN, preferred_element_type=F32
            )
            mean_ref[part, :] = lax.dot_general(
                wide, key_ref[...], TN, preferred_element_type=F32
            ).astype(BF16)

    column = pl.BlockSpec((rows, HEAD), lambda h: (0, h))
    entry_column = pl.BlockSpec((key_rows, HEAD), lambda h: (0, h))
    return pl.pallas_call(
        body,
        grid=(heads,),
        out_shape=(
            jax.ShapeDtypeStruct((heads, LANES, rows), F32),
            jax.ShapeDtypeStruct((heads, rows), F32),
            jax.ShapeDtypeStruct((rows, cols), F32),
            jax.ShapeDtypeStruct((rows, cols), BF16),
        ),
        in_specs=[
            pl.BlockSpec((rows, HEAD), lambda h: (0, h)),
            entry_column,
            entry_column,
            pl.BlockSpec((1, rows), lambda h: (0, 0)),
        ],
        out_specs=(
            pl.BlockSpec((1, LANES, rows), lambda h: (h, 0, 0)),
            pl.BlockSpec((heads, rows), lambda h: (0, 0)),
            column,
            column,
        ),
        name="local_softmax",
        **vmem_params(moved=1, mib=60),
    )(query_rows, keys, values, entry_lanes)


def partner_lanes(partner_ref, all_ref, out_ref, slots):
    heads = out_ref.shape[0]
    lane = lax.broadcasted_iota(jnp.int32, (heads, LANES), 1)
    for group in range(slots // 2):
        halves = []
        for half in range(2):
            slot = group * 2 + half
            device, there = partner_ref[0, slot], partner_ref[1, slot]
            start = pl.multiple_of(there // 2 * LANES, LANES)
            tile = all_ref[device, :, pl.ds(start, LANES)]
            turned = pltpu.roll(tile, BLOCK, 1)
            halves.append(jnp.where(there % 2 == half, tile, turned))
        out_ref[:, group * LANES : (group + 1) * LANES] = jnp.where(
            lane < BLOCK, halves[0], halves[1]
        )


def live_lanes(partner_ref, all_ref, out_ref, slots, rows):
    lane = lax.broadcasted_iota(jnp.int32, (1, LANES), 1)
    row = lax.broadcasted_iota(jnp.int32, (all_ref.shape[1], LANES), 0)
    for group in range(slots // 2):
        own, other = [], []
        for half in range(2):
            slot = group * 2 + half
            reader, place = partner_ref[2, slot], partner_ref[3, slot]
            counts = all_ref[reader, :, rows:]
            count = jnp.sum(
                jnp.where(row == place // NEIGH, counts, 0.0), axis=0, keepdims=True
            )
            at = (place % NEIGH).astype(F32)
            filled = partner_ref[4, slot] > 0
            own.append(jnp.where((at < count) & filled, 1.0, 0.0))
            other.append(jnp.where(NEIGH - 1 - at < count, 1.0, 0.0))
        part = slice(group * LANES, (group + 1) * LANES)
        out_ref[0:1, part] = jnp.where(lane < BLOCK, own[0], own[1])
        out_ref[1:2, part] = jnp.where(lane < BLOCK, other[0], other[1])


def head_columns(heads, cols):
    row = lax.broadcasted_iota(jnp.int32, (heads, cols), 0)
    column = lax.broadcasted_iota(jnp.int32, (heads, cols), 1)
    return jnp.where(row == column // HEAD, 1.0, 0.0).astype(BF16)


def row_dots(n_seq, lse, seen, grad_rows, count_lanes):
    heads, rows = lse.shape
    cols = seen.shape[1]
    step_rows = rows // STEPS
    steps = rows // step_rows

    def body(lse_ref, seen_ref, grad_ref, count_ref, all_ref, told_ref):
        step = pl.program_id(0)

        @pl.when(step == 0)
        def _():
            told_ref[:heads, :rows] = lse_ref[...]
            told_ref[:, rows:] = count_ref[...]

        terms = grad_ref[...].astype(F32) * seen_ref[...]
        high = terms.astype(BF16)
        low = (terms - high.astype(F32)).astype(BF16)
        of_head = head_columns(heads, cols)
        at = pl.ds(pl.multiple_of(step * step_rows, step_rows), step_rows)
        told_ref[heads:, at] = sum(
            lax.dot_general(of_head, part, NT, preferred_element_type=F32) for part in (high, low)
        )

        @pl.when(step == steps - 1)
        def _():
            for device in range(n_seq):
                all_ref[device] = told_ref[...]

    return pl.pallas_call(
        body,
        grid=(steps,),
        out_shape=jax.ShapeDtypeStruct((n_seq, 2 * heads, rows + LANES), F32),
        in_specs=[
            pl.BlockSpec((heads, rows), lambda i: (0, 0)),
            pl.BlockSpec((step_rows, cols), lambda i: (i, 0)),
            pl.BlockSpec((step_rows, cols), lambda i: (i, 0)),
            pl.BlockSpec((2 * heads, LANES), lambda i: (0, 0)),
        ],
        out_specs=pl.BlockSpec((n_seq, 2 * heads, rows + LANES), lambda i: (0, 0, 0)),
        scratch_shapes=[pltpu.VMEM((2 * heads, rows + LANES), F32)],
        name="row_dots",
        **vmem_params(moved=1, mib=60),
    )(lse, seen, grad_rows, count_lanes)


def slope_terms(weights, told, grad_rows, keys, values, entry_lanes):
    heads, _, rows = weights.shape
    cols = heads * HEAD
    key_rows = keys.shape[0]

    def body(weight_ref, told_ref, grad_ref, key_ref, value_ref, entry_ref, out_ref):
        head = pl.program_id(0)
        for part in lane_parts(rows):
            entry = entry_ref[:, part]
            slope = lax.dot_general(
                value_ref[...], grad_ref[part, :], NT, preferred_element_type=F32
            )
            dot = told_ref[0, pl.ds(heads + head, 1), part]
            terms = weight_ref[0, :, part] * (pick_entry(slope, entry) - dot)
            wide = spread_entry(terms, entry, key_rows // LANES)
            out_ref[part, :] = lax.dot_general(
                wide, key_ref[...], TN, preferred_element_type=F32
            ).astype(BF16)

    column = pl.BlockSpec((rows, HEAD), lambda h: (0, h))
    entry_column = pl.BlockSpec((key_rows, HEAD), lambda h: (0, h))
    return pl.pallas_call(
        body,
        grid=(heads,),
        out_shape=jax.ShapeDtypeStruct((rows, cols), BF16),
        in_specs=[
            pl.BlockSpec((1, LANES, rows), lambda h: (h, 0, 0)),
            pl.BlockSpec((1,) + told.shape[1:], lambda h: (0, 0, 0)),
            pl.BlockSpec((rows, HEAD), lambda h: (0, h)),
            entry_column,
            entry_column,
            pl.BlockSpec((1, rows), lambda h: (0, 0)),
        ],
        out_specs=column,
        name="slope_terms",
        **vmem_params(moved=1, mib=60),
    )(weights, told, grad_rows, keys, values, entry_lanes)


def query_terms_of(terms, mean, all_told, my_index, partner):
    rows, cols = terms.shape
    heads = cols // HEAD
    slots = rows // BLOCK
    step_rows = rows // STEPS
    scale = 1.0 / math.sqrt(HEAD)

    def body(
        partner_ref, index_ref, all_ref, term_ref, mean_ref, stat_ref, out_ref, other_ref, live_ref, more_ref
    ):
        step = pl.program_id(0)

        @pl.when(step == 0)
        def _():
            partner_lanes(partner_ref, all_ref, other_ref, slots)
            live_lanes(partner_ref, all_ref, live_ref, slots, rows)
            own = all_ref[index_ref[0], :, :rows]
            apart = other_ref[:heads, :] - own[:heads, :]
            own_live, other_live = live_ref[0:1, :] > 0.0, live_ref[1:2, :] > 0.0
            odds = jnp.where(other_live, jnp.exp(apart), 0.0)
            share = jnp.where(own_live, 1.0 / (1.0 + odds), 0.0)
            rest = jnp.where(other_live, 1.0 / (1.0 + jnp.exp(-apart)), 0.0)
            more = rest * (other_ref[heads:, :] - own[heads:, :])
            stat_ref[:heads, :] = share
            stat_ref[heads:, :] = own[heads:, :] + more
            more_ref[...] = more

        at = pl.ds(pl.multiple_of(step * step_rows, step_rows), step_rows)
        of_head = head_columns(heads, cols)

        def spread(rows_of_heads):
            high = rows_of_heads.astype(BF16)
            low = (rows_of_heads - high.astype(F32)).astype(BF16)
            return sum(
                lax.dot_general(part, of_head, TN, preferred_element_type=F32)
                for part in (high, low)
            )

        share, more = spread(stat_ref[:heads, at]), spread(more_ref[:, at])
        query = share * (term_ref[...].astype(F32) - more * mean_ref[...].astype(F32))
        out_ref[...] = (query * scale).astype(BF16)

    block = pl.BlockSpec((step_rows, cols), lambda i: (i, 0))
    return pl.pallas_call(
        body,
        grid=(rows // step_rows,),
        out_shape=(
            jax.ShapeDtypeStruct((2 * heads, rows), F32),
            jax.ShapeDtypeStruct((rows, cols), BF16),
        ),
        in_specs=[
            pl.BlockSpec(memory_space=pltpu.SMEM),
            pl.BlockSpec(memory_space=pltpu.SMEM),
            pl.BlockSpec(all_told.shape, lambda i: (0, 0, 0)),
            pl.BlockSpec((step_rows, cols), lambda i: (i, 0)),
            pl.BlockSpec((step_rows, cols), lambda i: (i, 0)),
        ],
        out_specs=(pl.BlockSpec((2 * heads, rows), lambda i: (0, 0)), block),
        scratch_shapes=[
            pltpu.VMEM((2 * heads, rows), F32),
            pltpu.VMEM((2, rows), F32),
            pltpu.VMEM((heads, rows), F32),
        ],
        name="query_terms",
        **vmem_params(moved=1, mib=60),
    )(partner, my_index, all_told, terms, mean)


def entry_grads(weights, stat, query_rows, grad_rows, values, entry_lanes):
    heads, _, rows = weights.shape
    cols = heads * HEAD
    entry_rows = values.shape[0]
    scale = 1.0 / math.sqrt(HEAD)

    def body(weight_ref, stat_ref, query_ref, grad_ref, value_ref, entry_ref, key_out, value_out):
        head = pl.program_id(0)
        key_sum = jnp.zeros((entry_rows, HEAD), F32)
        value_sum = jnp.zeros((entry_rows, HEAD), F32)
        for part in lane_parts(rows):
            entry = entry_ref[:, part]
            grad = grad_ref[part, :]
            joint = weight_ref[0, :, part] * stat_ref[pl.ds(head, 1), part]
            slope = lax.dot_general(value_ref[...], grad, NT, preferred_element_type=F32)
            low = joint * (pick_entry(slope, entry) - stat_ref[pl.ds(heads + head, 1), part])
            wide = spread_entry(joint, entry, entry_rows // LANES)
            value_sum += lax.dot_general(wide, grad, NN, preferred_element_type=F32)
            wide = spread_entry(low, entry, entry_rows // LANES)
            key_sum += lax.dot_general(wide, query_ref[part, :], NN, preferred_element_type=F32)
        key_out[...] = (key_sum * scale).astype(BF16)
        value_out[...] = value_sum.astype(BF16)

    entry_column = pl.BlockSpec((entry_rows, HEAD), lambda h: (0, h))
    return pl.pallas_call(
        body,
        grid=(heads,),
        out_shape=[jax.ShapeDtypeStruct((entry_rows, cols), BF16)] * 2,
        in_specs=[
            pl.BlockSpec((1, LANES, rows), lambda h: (h, 0, 0)),
            pl.BlockSpec((2 * heads, rows), lambda h: (0, 0)),
            pl.BlockSpec((rows, HEAD), lambda h: (0, h)),
            pl.BlockSpec((rows, HEAD), lambda h: (0, h)),
            pl.BlockSpec((entry_rows, HEAD), lambda h: (0, h)),
            pl.BlockSpec((1, rows), lambda h: (0, 0)),
        ],
        out_specs=[entry_column] * 2,
        name="entry_grads",
        **vmem_params(moved=1, mib=60),
    )(weights, stat, query_rows, grad_rows, values, entry_lanes)


def swap(value, axis, bits):
    size = lax.axis_size(axis)
    return lax.ppermute(value, axis, [(i, i ^ bits) for i in range(size)])


def rank_slots(owners):
    slot_total = owners.shape[-1]
    earlier_mask = jnp.arange(slot_total)[None, :] < jnp.arange(slot_total)[:, None]
    same_owner = owners[..., :, None] == owners[..., None, :]
    return jnp.sum(same_owner & earlier_mask, axis=-1)


def owner_tables(all_lists, my_index, entries_here, slot_cap):
    n_seq, places = all_lists.shape
    owners = all_lists // entries_here
    ranks = rank_slots(owners)
    chosen = (owners == my_index)[:, None, :] & (
        ranks[:, None, :] == jnp.arange(slot_cap)[None, :, None]
    )

    def look(table):
        return jnp.sum(jnp.where(chosen, table[:, None, :], 0), axis=2).reshape(-1)

    def other(table):
        return table.reshape(n_seq, -1, NEIGH)[:, :, ::-1].reshape(n_seq, places)

    reader = jnp.arange(n_seq)[:, None]
    partner = [
        look(other(owners)),
        look(other(ranks) + slot_cap * reader),
        look(reader + jnp.zeros_like(owners)),
        look(jnp.arange(places) + jnp.zeros_like(owners)),
        look(jnp.ones_like(owners)),
    ]
    entry = look(all_lists % entries_here)
    return (
        jnp.repeat(entry[None], BLOCK, axis=1).astype(jnp.int32),
        jnp.stack(partner).astype(jnp.int32),
    )


def on_device(out_grad, out_weight, queries, keys, values, retrieval, counts):
    n_seq, n_mp = lax.axis_size("seq"), lax.axis_size("mp")
    my_index, my_mp = lax.axis_index("seq"), lax.axis_index("mp")
    tok_rows, head_cols = queries.shape
    entries_here, nbr_rows, _ = keys.shape
    blocks_here = tok_rows // BLOCK
    places = blocks_here * NEIGH
    slot_cap = (places + n_seq - 1) // n_seq
    rows = n_seq * slot_cap * BLOCK
    feats = out_grad.shape[1]
    lists = retrieval
    index_arr = my_index.astype(jnp.int32).reshape(1)
    key_rows = keys.reshape(entries_here * nbr_rows, head_cols)
    value_rows = values.reshape(entries_here * nbr_rows, head_cols)

    def exchange(slot_rows):
        cols = slot_rows.shape[-1]
        return lax.all_to_all(
            slot_rows.reshape(n_seq, slot_cap * BLOCK, cols), "seq", 0, 0, tiled=True
        ).reshape(rows, cols)

    far_bits = list(range(2, n_mp, 2))
    tie = lax.optimization_barrier
    far = [swap(out_grad, "mp", bits) for bits in far_bits]
    near = swap(out_grad, "mp", 1)
    query_places = place_rows(queries, lists, index_arr, n_seq, slot_cap, entries_here)
    query_slots = exchange(query_places)
    entry_lanes, partner = owner_tables(
        retrieval.reshape(n_seq, places), my_index, entries_here, slot_cap
    )

    placing = (lists, index_arr, n_seq, slot_cap, entries_here, HEAD_CHUNKS)
    (grad_sum,) = add_product(None, [out_grad, near], out_weight, [(my_mp, 0), (my_mp ^ 1, 0)])
    far, grad_sum = tie((far, grad_sum))
    beside = [swap(part, "mp", 1) for part in far]
    (grad_sum,) = add_product(grad_sum, far, out_weight, [(my_mp ^ bits, 0) for bits in far_bits])
    beside, grad_sum = tie((beside, grad_sum))
    grad_sum = add_product(
        grad_sum, beside, out_weight, [(my_mp ^ bits ^ 1, 0) for bits in far_bits], placing
    )
    grad_places = grad_sum

    count_lanes = jnp.pad(counts.astype(F32), (0, max(0, 2 * head_cols // HEAD - blocks_here)))
    count_lanes = jnp.broadcast_to(count_lanes[:, None], (count_lanes.shape[0], LANES))
    weights, lse, seen, mean = local_softmax(query_slots, key_rows, value_rows, entry_lanes)
    grad_slots = exchange(grad_places[0])
    weights, lse, seen, mean, grad_slots = tie((weights, lse, seen, mean, grad_slots))
    told = row_dots(n_seq, lse, seen, grad_slots, count_lanes)
    all_told = lax.all_to_all(told, "seq", 0, 0, tiled=True)
    terms = slope_terms(weights, told, grad_slots, key_rows, value_rows, entry_lanes)
    all_told, terms = tie((all_told, terms))
    stat, query_terms = query_terms_of(terms, mean, all_told, index_arr, partner)
    back = exchange(query_terms).reshape(-1, BLOCK, head_cols)
    query_grad = join_places(
        0, 1, back, None, lists, index_arr, n_seq, slot_cap, entries_here, blocks_here
    )
    key_grad, value_grad = entry_grads(
        weights, stat, query_slots, grad_slots, value_rows, entry_lanes
    )
    key_grad = key_grad.reshape(keys.shape)
    value_grad = value_grad.reshape(values.shape)
    return (query_grad, key_grad, value_grad)


def solution(mesh):
    return jax.shard_map(
        on_device,
        mesh=mesh,
        in_specs=(
            P("seq", "mp"),
            P("mp", None),
            P("seq", "mp"),
            P("seq", None, "mp"),
            P("seq", None, "mp"),
            P(),
            P("seq"),
        ),
        out_specs=(P("seq", "mp"), P("seq", None, "mp"), P("seq", None, "mp")),
        check_vma=False,
    )
```

```python
import functools
import math

import jax
import jax.numpy as jnp
from jax import lax
from jax.experimental import pallas as pl
from jax.experimental.pallas import tpu as pltpu
from jax.sharding import PartitionSpec as P

HEAD = 128
BLOCK = 64
NEIGH = 2
LANES = 128
HEAD_CHUNKS = 1
STEPS = 2
F32 = jnp.float32
BF16 = jnp.bfloat16


def vmem_params(flops=0, moved=0, mib=48):
    return dict(
        compiler_params=pltpu.CompilerParams(vmem_limit_bytes=mib * 1024 * 1024),
        cost_estimate=pl.CostEstimate(flops=flops, bytes_accessed=moved, transcendentals=0),
    )


def slot_of_place(lists_ref, base, place, entries_here, slot_cap):
    owner = lists_ref[base + place // NEIGH, place % NEIGH] // entries_here
    rank = 0
    for earlier in range(place):
        named = lists_ref[base + earlier // NEIGH, earlier % NEIGH]
        rank = rank + jnp.where(named // entries_here == owner, 1, 0)
    return owner * slot_cap + rank


def place_copies(lists_ref, base, rows_ref, out_refs, zero_ref, sems, places, entries_here, slot_cap):
    slots = out_refs[0].shape[0]
    width = out_refs[0].shape[2]
    if slots > places:
        zero_ref[...] = jnp.zeros_like(zero_ref)
        for chunk, out_ref in enumerate(out_refs):
            blanks = [
                pltpu.make_async_copy(zero_ref, out_ref.at[slot], sems.at[chunk, slot])
                for slot in range(slots)
            ]
            for blank in blanks:
                blank.start()
            for blank in blanks:
                blank.wait()
    slot_list = [
        slot_of_place(lists_ref, base, place, entries_here, slot_cap) for place in range(places)
    ]
    copies = []
    for chunk, out_ref in enumerate(out_refs):
        for place, slot in enumerate(slot_list):
            start = place // NEIGH * BLOCK
            copies.append(
                pltpu.make_async_copy(
                    rows_ref.at[pl.ds(start, BLOCK), pl.ds(chunk * width, width)],
                    out_ref.at[slot],
                    sems.at[chunk, place],
                )
            )
            copies[-1].start()
    for copy in copies:
        copy.wait()


def place_rows(rows, lists, my_index, n_seq, slot_cap, entries_here):
    tok_rows, cols = rows.shape
    places = tok_rows // BLOCK * NEIGH
    slots = n_seq * slot_cap

    def body(lists_ref, index_ref, rows_ref, out_ref, zero_ref, sems):
        place_copies(
            lists_ref,
            index_ref[0] * (places // NEIGH),
            rows_ref,
            [out_ref],
            zero_ref,
            sems,
            places,
            entries_here,
            slot_cap,
        )

    return pl.pallas_call(
        body,
        out_shape=jax.ShapeDtypeStruct((slots, BLOCK, cols), rows.dtype),
        in_specs=[
            pl.BlockSpec(memory_space=pltpu.SMEM),
            pl.BlockSpec(memory_space=pltpu.SMEM),
            pl.BlockSpec(memory_space=pltpu.VMEM),
        ],
        out_specs=pl.BlockSpec(memory_space=pl.ANY),
        scratch_shapes=[
            pltpu.VMEM((BLOCK, cols), rows.dtype),
            pltpu.SemaphoreType.DMA((1, max(slots, places))),
        ],
        name="place_rows",
        **vmem_params(moved=2 * slots * BLOCK * cols * 2, mib=60),
    )(lists, my_index, rows)


def add_product(total, parts, weight, sources, placing=None):
    tok_rows, width = parts[0].shape
    feats = weight.shape[1] // lax.axis_size("mp")
    unit = math.gcd(width, feats)
    cuts = range(width // unit)
    first_units = [source * (feats // unit) + at // unit for source, at in sources]
    cols = weight.shape[0]
    step_cols = cols // (2 * len(parts)) if len(parts) < 3 else min(256, cols)
    steps = cols // step_cols
    places = tok_rows // BLOCK * NEIGH
    before = [] if total is None else [total]
    if placing is None:
        chunks = 1
    else:
        lists, my_index, n_seq, slot_cap, entries_here, chunks = placing
        slots = n_seq * slot_cap

    def body(source_ref, *refs):
        refs = list(refs)
        place_refs = [refs.pop(0) for _ in range(2)] if placing is not None else None
        before_ref = refs.pop(0) if before else None
        part_refs = [refs.pop(0) for _ in parts]
        weight_refs = [[refs.pop(0) for _ in cuts] for _ in parts]
        out_refs = [refs.pop(0) for _ in range(chunks)]
        step = pl.program_id(0)
        result = before_ref[...] if before else 0.0
        for part_ref, weight_cuts in zip(part_refs, weight_refs):
            for cut, weight_ref in zip(cuts, weight_cuts):
                result = result + lax.dot_general(
                    part_ref[:, cut * unit : (cut + 1) * unit],
                    weight_ref[...],
                    NT,
                    preferred_element_type=F32,
                )
        if placing is None:
            out_refs[0][...] = result
            return
        low_ref, zero_ref, sems = refs
        low_ref[:, pl.ds(pl.multiple_of(step * step_cols, step_cols), step_cols)] = result.astype(
            BF16
        )

        @pl.when(step == steps - 1)
        def _():
            lists_ref, index_ref = place_refs
            place_copies(
                lists_ref,
                index_ref[0] * (places // NEIGH),
                low_ref,
                out_refs,
                zero_ref,
                sems,
                places,
                entries_here,
                slot_cap,
            )

    block = pl.BlockSpec((tok_rows, step_cols), lambda k, s: (0, k))
    in_specs = [block] * len(before)
    in_specs += [pl.BlockSpec((tok_rows, width), lambda k, s: (0, 0))] * len(parts)
    for number in range(len(parts)):
        for cut in cuts:
            in_specs.append(
                pl.BlockSpec((step_cols, unit), lambda k, s, n=number, c=cut: (k, s[n] + c))
            )
    if placing is None:
        out_shape, out_specs = [jax.ShapeDtypeStruct((tok_rows, cols), F32)], [block]
        scratch, extra = [], []
    else:
        chunk_cols = cols // chunks
        out_shape = [jax.ShapeDtypeStruct((slots, BLOCK, chunk_cols), BF16)] * chunks
        out_specs = [pl.BlockSpec(memory_space=pl.ANY)] * chunks
        scratch = [
            pltpu.VMEM((tok_rows, cols), BF16),
            pltpu.VMEM((BLOCK, chunk_cols), BF16),
            pltpu.SemaphoreType.DMA((chunks, max(slots, places))),
        ]
        extra = [lists, my_index]
        in_specs = [pl.BlockSpec(memory_space=pltpu.SMEM)] * 2 + in_specs
    return pl.pallas_call(
        body,
        grid_spec=pltpu.PrefetchScalarGridSpec(
            num_scalar_prefetch=1,
            grid=(steps,),
            in_specs=in_specs,
            out_specs=out_specs,
            scratch_shapes=scratch,
        ),
        out_shape=out_shape,
        name="add_product",
        **vmem_params(moved=1, mib=60),
    )(
        jnp.stack(first_units).astype(jnp.int32),
        *extra,
        *before,
        *parts,
        *[weight] * (len(parts) * len(cuts)),
    )


def join_places(
    chunk, chunks, back, before, lists, my_index, n_seq, slot_cap, entries_here, blocks_here
):
    slots, _, cols = back.shape
    places = blocks_here * NEIGH
    kept = [] if before is None else [before]

    def body(lists_ref, index_ref, back_ref, *refs):
        out_ref = refs[-1]
        base = index_ref[0] * (places // NEIGH)
        for block in range(blocks_here):
            total = 0.0
            for neighbour in range(NEIGH):
                slot = slot_of_place(
                    lists_ref, base, block * NEIGH + neighbour, entries_here, slot_cap
                )
                total = total + back_ref[slot].astype(F32)
            out_ref[block * BLOCK : (block + 1) * BLOCK, :] = total.astype(out_ref.dtype)

    return pl.pallas_call(
        body,
        grid=(1,),
        out_shape=jax.ShapeDtypeStruct((blocks_here * BLOCK, chunks * cols), back.dtype),
        in_specs=[
            pl.BlockSpec(memory_space=pltpu.SMEM),
            pl.BlockSpec(memory_space=pltpu.SMEM),
            pl.BlockSpec((slots, BLOCK, cols), lambda i: (0, 0, 0)),
        ]
        + [pl.BlockSpec(memory_space=pl.ANY)] * len(kept),
        out_specs=pl.BlockSpec((blocks_here * BLOCK, cols), lambda i: (0, chunk)),
        input_output_aliases={3: 0} if kept else {},
        name="join_places",
        **vmem_params(moved=3 * slots * BLOCK * cols),
    )(lists, my_index, back, *kept)


def lane_parts(total):
    width = math.gcd(total, 512)
    return [slice(at, at + width) for at in range(0, total, width)]


def pick_entry(stacked, entry):
    entries = stacked.shape[0] // LANES
    chosen = stacked[:LANES]
    for number in range(1, entries):
        chosen = jnp.where(
            entry == number, stacked[number * LANES : (number + 1) * LANES], chosen
        )
    return chosen


def spread_entry(chosen, entry, entries):
    return jnp.concatenate(
        [jnp.where(entry == number, chosen, 0.0) for number in range(entries)], axis=0
    ).astype(BF16)


NT = (((1,), (1,)), ((), ()))
NN = (((1,), (0,)), ((), ()))
TN = (((0,), (0,)), ((), ()))


def local_softmax(query_rows, keys, values, entry_lanes):
    rows, cols = query_rows.shape
    heads = cols // HEAD
    key_rows = keys.shape[0]
    scale = 1.0 / math.sqrt(HEAD)

    def body(query_ref, key_ref, value_ref, entry_ref, weight_ref, lse_ref, seen_ref, mean_ref):
        head = pl.program_id(0)
        for part in lane_parts(rows):
            entry = entry_ref[:, part]
            scores = lax.dot_general(
                key_ref[...], query_ref[part, :], NT, preferred_element_type=F32
            )
            scores = pick_entry(scores, entry) * scale
            top = jnp.max(scores, axis=0, keepdims=True)
            raised = jnp.exp(scores - top)
            total = jnp.sum(raised, axis=0, keepdims=True)
            weights = raised / total
            weight_ref[0, :, part] = weights
            lse_ref[pl.ds(head, 1), part] = top + jnp.log(total)
            wide = spread_entry(weights, entry, key_rows // LANES)
            seen_ref[part, :] = lax.dot_general(
                wide, value_ref[...], TN, preferred_element_type=F32
            )
            mean_ref[part, :] = lax.dot_general(
                wide, key_ref[...], TN, preferred_element_type=F32
            ).astype(BF16)

    column = pl.BlockSpec((rows, HEAD), lambda h: (0, h))
    entry_column = pl.BlockSpec((key_rows, HEAD), lambda h: (0, h))
    return pl.pallas_call(
        body,
        grid=(heads,),
        out_shape=(
            jax.ShapeDtypeStruct((heads, LANES, rows), F32),
            jax.ShapeDtypeStruct((heads, rows), F32),
            jax.ShapeDtypeStruct((rows, cols), F32),
            jax.ShapeDtypeStruct((rows, cols), BF16),
        ),
        in_specs=[
            pl.BlockSpec((rows, HEAD), lambda h: (0, h)),
            entry_column,
            entry_column,
            pl.BlockSpec((1, rows), lambda h: (0, 0)),
        ],
        out_specs=(
            pl.BlockSpec((1, LANES, rows), lambda h: (h, 0, 0)),
            pl.BlockSpec((heads, rows), lambda h: (0, 0)),
            column,
            column,
        ),
        name="local_softmax",
        **vmem_params(moved=1, mib=60),
    )(query_rows, keys, values, entry_lanes)


def partner_lanes(partner_ref, device_row, all_ref, out_ref, slots):
    heads = out_ref.shape[0]
    lane = lax.broadcasted_iota(jnp.int32, (heads, LANES), 1)
    for group in range(slots // 2):
        halves = []
        for half in range(2):
            slot = group * 2 + half
            device, there = partner_ref[device_row, slot], partner_ref[1, slot]
            start = pl.multiple_of(there // 2 * LANES, LANES)
            tile = all_ref[device, :, pl.ds(start, LANES)]
            turned = pltpu.roll(tile, BLOCK, 1)
            halves.append(jnp.where(there % 2 == half, tile, turned))
        out_ref[:, group * LANES : (group + 1) * LANES] = jnp.where(
            lane < BLOCK, halves[0], halves[1]
        )


def live_lanes(partner_ref, all_ref, out_ref, slots, rows):
    lane = lax.broadcasted_iota(jnp.int32, (1, LANES), 1)
    for group in range(slots // 2):
        own, other = [], []
        for half in range(2):
            slot = group * 2 + half
            reader, place = partner_ref[2, slot], partner_ref[3, slot]
            counts = all_ref[reader, 0:1, rows:]
            count = jnp.sum(
                jnp.where(lane == place // NEIGH, counts, 0.0), axis=1, keepdims=True
            )
            at = (place % NEIGH).astype(F32)
            filled = partner_ref[4, slot] > 0
            own.append(jnp.where((at < count) & filled, 1.0, 0.0))
            other.append(jnp.where(NEIGH - 1 - at < count, 1.0, 0.0))
        part = slice(group * LANES, (group + 1) * LANES)
        out_ref[0:1, part] = jnp.where(lane < BLOCK, own[0], own[1])
        out_ref[1:2, part] = jnp.where(lane < BLOCK, other[0], other[1])


def head_columns(heads, cols):
    row = lax.broadcasted_iota(jnp.int32, (heads, cols), 0)
    column = lax.broadcasted_iota(jnp.int32, (heads, cols), 1)
    return jnp.where(row == column // HEAD, 1.0, 0.0).astype(BF16)


def row_dots(n_seq, seen, grad_rows):
    rows, cols = seen.shape
    heads = cols // HEAD
    step_rows = rows // STEPS
    steps = rows // step_rows

    def body(seen_ref, grad_ref, all_ref, told_ref):
        step = pl.program_id(0)
        terms = grad_ref[...].astype(F32) * seen_ref[...]
        high = terms.astype(BF16)
        low = (terms - high.astype(F32)).astype(BF16)
        of_head = head_columns(heads, cols)
        at = pl.ds(pl.multiple_of(step * step_rows, step_rows), step_rows)
        told_ref[:, at] = sum(
            lax.dot_general(of_head, part, NT, preferred_element_type=F32) for part in (high, low)
        )

        @pl.when(step == steps - 1)
        def _():
            for device in range(n_seq):
                all_ref[device] = told_ref[...]

    return pl.pallas_call(
        body,
        grid=(steps,),
        out_shape=jax.ShapeDtypeStruct((n_seq, heads, rows), F32),
        in_specs=[
            pl.BlockSpec((step_rows, cols), lambda i: (i, 0)),
            pl.BlockSpec((step_rows, cols), lambda i: (i, 0)),
        ],
        out_specs=pl.BlockSpec((n_seq, heads, rows), lambda i: (0, 0, 0)),
        scratch_shapes=[pltpu.VMEM((heads, rows), F32)],
        name="row_dots",
        **vmem_params(moved=1, mib=60),
    )(seen, grad_rows)


def slope_terms(weights, told, grad_rows, keys, values, entry_lanes):
    heads, _, rows = weights.shape
    cols = heads * HEAD
    key_rows = keys.shape[0]

    def body(weight_ref, told_ref, grad_ref, key_ref, value_ref, entry_ref, out_ref):
        head = pl.program_id(0)
        for part in lane_parts(rows):
            entry = entry_ref[:, part]
            slope = lax.dot_general(
                value_ref[...], grad_ref[part, :], NT, preferred_element_type=F32
            )
            dot = told_ref[0, pl.ds(head, 1), part]
            terms = weight_ref[0, :, part] * (pick_entry(slope, entry) - dot)
            wide = spread_entry(terms, entry, key_rows // LANES)
            out_ref[part, :] = lax.dot_general(
                wide, key_ref[...], TN, preferred_element_type=F32
            ).astype(BF16)

    column = pl.BlockSpec((rows, HEAD), lambda h: (0, h))
    entry_column = pl.BlockSpec((key_rows, HEAD), lambda h: (0, h))
    return pl.pallas_call(
        body,
        grid=(heads,),
        out_shape=jax.ShapeDtypeStruct((rows, cols), BF16),
        in_specs=[
            pl.BlockSpec((1, LANES, rows), lambda h: (h, 0, 0)),
            pl.BlockSpec((1,) + told.shape[1:], lambda h: (0, 0, 0)),
            pl.BlockSpec((rows, HEAD), lambda h: (0, h)),
            entry_column,
            entry_column,
            pl.BlockSpec((1, rows), lambda h: (0, 0)),
        ],
        out_specs=column,
        name="slope_terms",
        **vmem_params(moved=1, mib=60),
    )(weights, told, grad_rows, keys, values, entry_lanes)


def query_terms_of(terms, mean, lse, dots, all_lse, all_dots, partner):
    rows, cols = terms.shape
    heads = cols // HEAD
    slots = rows // BLOCK
    step_rows = rows // STEPS
    scale = 1.0 / math.sqrt(HEAD)

    def body(partner_ref, lse_ref, dot_ref, all_lse_ref, all_dot_ref, term_ref, mean_ref, *refs):
        stat_ref, out_ref, other_ref, apart_ref, live_ref, more_ref = refs
        step = pl.program_id(0)

        @pl.when(step == 0)
        def _():
            partner_lanes(partner_ref, 5, all_lse_ref, apart_ref, slots)
            partner_lanes(partner_ref, 0, all_dot_ref, other_ref, slots)
            live_lanes(partner_ref, all_lse_ref, live_ref, slots, rows)
            own = dot_ref[0]
            apart = apart_ref[...] - lse_ref[...]
            own_live, other_live = live_ref[0:1, :] > 0.0, live_ref[1:2, :] > 0.0
            odds = jnp.where(other_live, jnp.exp(apart), 0.0)
            share = jnp.where(own_live, 1.0 / (1.0 + odds), 0.0)
            rest = jnp.where(other_live, 1.0 / (1.0 + jnp.exp(-apart)), 0.0)
            more = rest * (other_ref[...] - own)
            stat_ref[:heads, :] = share
            stat_ref[heads:, :] = own + more
            more_ref[...] = more

        at = pl.ds(pl.multiple_of(step * step_rows, step_rows), step_rows)
        of_head = jnp.concatenate([head_columns(heads, cols)] * 2, axis=0)

        def spread(rows_of_heads):
            high = rows_of_heads.astype(BF16)
            low = (rows_of_heads - high.astype(F32)).astype(BF16)
            return lax.dot_general(
                jnp.concatenate([high, low], axis=0), of_head, TN, preferred_element_type=F32
            )

        share, more = spread(stat_ref[:heads, at]), spread(more_ref[:, at])
        query = share * (term_ref[...].astype(F32) - more * mean_ref[...].astype(F32))
        out_ref[...] = (query * scale).astype(BF16)

    block = pl.BlockSpec((step_rows, cols), lambda i: (i, 0))
    return pl.pallas_call(
        body,
        grid=(rows // step_rows,),
        out_shape=(
            jax.ShapeDtypeStruct((2 * heads, rows), F32),
            jax.ShapeDtypeStruct((rows, cols), BF16),
        ),
        in_specs=[
            pl.BlockSpec(memory_space=pltpu.SMEM),
            pl.BlockSpec((heads, rows), lambda i: (0, 0)),
            pl.BlockSpec((1, heads, rows), lambda i: (0, 0, 0)),
            pl.BlockSpec(all_lse.shape, lambda i: (0, 0, 0)),
            pl.BlockSpec(all_dots.shape, lambda i: (0, 0, 0)),
            pl.BlockSpec((step_rows, cols), lambda i: (i, 0)),
            pl.BlockSpec((step_rows, cols), lambda i: (i, 0)),
        ],
        out_specs=(pl.BlockSpec((2 * heads, rows), lambda i: (0, 0)), block),
        scratch_shapes=[
            pltpu.VMEM((heads, rows), F32),
            pltpu.VMEM((heads, rows), F32),
            pltpu.VMEM((2, rows), F32),
            pltpu.VMEM((heads, rows), F32),
        ],
        name="query_terms",
        **vmem_params(moved=1, mib=60),
    )(partner, lse, dots, all_lse, all_dots, terms, mean)


def entry_grads(weights, stat, query_rows, grad_rows, values, entry_lanes):
    heads, _, rows = weights.shape
    cols = heads * HEAD
    entry_rows = values.shape[0]
    scale = 1.0 / math.sqrt(HEAD)

    def body(weight_ref, stat_ref, query_ref, grad_ref, value_ref, entry_ref, key_out, value_out):
        head = pl.program_id(0)
        key_sum = jnp.zeros((entry_rows, HEAD), F32)
        value_sum = jnp.zeros((entry_rows, HEAD), F32)
        for part in lane_parts(rows):
            entry = entry_ref[:, part]
            grad = grad_ref[part, :]
            joint = weight_ref[0, :, part] * stat_ref[pl.ds(head, 1), part]
            slope = lax.dot_general(value_ref[...], grad, NT, preferred_element_type=F32)
            low = joint * (pick_entry(slope, entry) - stat_ref[pl.ds(heads + head, 1), part])
            wide = spread_entry(joint, entry, entry_rows // LANES)
            value_sum += lax.dot_general(wide, grad, NN, preferred_element_type=F32)
            wide = spread_entry(low, entry, entry_rows // LANES)
            key_sum += lax.dot_general(wide, query_ref[part, :], NN, preferred_element_type=F32)
        key_out[...] = (key_sum * scale).astype(BF16)
        value_out[...] = value_sum.astype(BF16)

    entry_column = pl.BlockSpec((entry_rows, HEAD), lambda h: (0, h))
    return pl.pallas_call(
        body,
        grid=(heads,),
        out_shape=[jax.ShapeDtypeStruct((entry_rows, cols), BF16)] * 2,
        in_specs=[
            pl.BlockSpec((1, LANES, rows), lambda h: (h, 0, 0)),
            pl.BlockSpec((2 * heads, rows), lambda h: (0, 0)),
            pl.BlockSpec((rows, HEAD), lambda h: (0, h)),
            pl.BlockSpec((rows, HEAD), lambda h: (0, h)),
            pl.BlockSpec((entry_rows, HEAD), lambda h: (0, h)),
            pl.BlockSpec((1, rows), lambda h: (0, 0)),
        ],
        out_specs=[entry_column] * 2,
        name="entry_grads",
        **vmem_params(moved=1, mib=60),
    )(weights, stat, query_rows, grad_rows, values, entry_lanes)


def swap(value, axis, bits):
    size = lax.axis_size(axis)
    return lax.ppermute(value, axis, [(i, i ^ bits) for i in range(size)])


def cube_gather(value, axis, steps):
    for step in steps:
        bits = lax.axis_size(axis) >> (step + 1)
        value = jnp.concatenate([value, swap(value, axis, bits)], axis=0)
    return value


def rank_slots(owners):
    slot_total = owners.shape[-1]
    earlier_mask = jnp.arange(slot_total)[None, :] < jnp.arange(slot_total)[:, None]
    same_owner = owners[..., :, None] == owners[..., None, :]
    return jnp.sum(same_owner & earlier_mask, axis=-1)


def owner_tables(all_lists, my_index, entries_here, slot_cap):
    n_seq, places = all_lists.shape
    owners = all_lists // entries_here
    ranks = rank_slots(owners)
    chosen = (owners == my_index)[:, None, :] & (
        ranks[:, None, :] == jnp.arange(slot_cap)[None, :, None]
    )

    def look(table):
        return jnp.sum(jnp.where(chosen, table[:, None, :], 0), axis=2).reshape(-1)

    def other(table):
        return table.reshape(n_seq, -1, NEIGH)[:, :, ::-1].reshape(n_seq, places)

    reader = jnp.arange(n_seq)[:, None]

    def turned(device):
        apart, position, bits = device ^ my_index, 0, n_seq >> 1
        for step in range(n_seq.bit_length() - 1):
            position = position + (apart >> step) % 2 * (bits >> step)
        return position

    partner = [
        look(other(owners)),
        look(other(ranks) + slot_cap * reader),
        look(turned(reader) + jnp.zeros_like(owners)),
        look(jnp.arange(places) + jnp.zeros_like(owners)),
        look(jnp.ones_like(owners)),
        look(turned(other(owners))),
    ]
    entry = look(all_lists % entries_here)
    return (
        jnp.repeat(entry[None], BLOCK, axis=1).astype(jnp.int32),
        jnp.stack(partner).astype(jnp.int32),
    )


def on_device(out_grad, out_weight, queries, keys, values, retrieval, counts):
    n_seq, n_mp = lax.axis_size("seq"), lax.axis_size("mp")
    my_index, my_mp = lax.axis_index("seq"), lax.axis_index("mp")
    tok_rows, head_cols = queries.shape
    entries_here, nbr_rows, _ = keys.shape
    blocks_here = tok_rows // BLOCK
    places = blocks_here * NEIGH
    slot_cap = (places + n_seq - 1) // n_seq
    rows = n_seq * slot_cap * BLOCK
    feats = out_grad.shape[1]
    lists = retrieval
    index_arr = my_index.astype(jnp.int32).reshape(1)
    key_rows = keys.reshape(entries_here * nbr_rows, head_cols)
    value_rows = values.reshape(entries_here * nbr_rows, head_cols)

    def exchange(slot_rows):
        cols = slot_rows.shape[-1]
        return lax.all_to_all(
            slot_rows.reshape(n_seq, slot_cap * BLOCK, cols), "seq", 0, 0, tiled=True
        ).reshape(rows, cols)

    far_bits = list(range(2, n_mp, 2))
    tie = lax.optimization_barrier
    far = [swap(out_grad, "mp", bits) for bits in far_bits]
    near = swap(out_grad, "mp", 1)
    query_places = place_rows(queries, lists, index_arr, n_seq, slot_cap, entries_here)
    query_slots = exchange(query_places)
    entry_lanes, partner = owner_tables(
        retrieval.reshape(n_seq, places), my_index, entries_here, slot_cap
    )

    placing = (lists, index_arr, n_seq, slot_cap, entries_here, HEAD_CHUNKS)
    (grad_sum,) = add_product(None, [out_grad, near], out_weight, [(my_mp, 0), (my_mp ^ 1, 0)])
    far, grad_sum = tie((far, grad_sum))
    beside = [swap(part, "mp", 1) for part in far]
    (grad_sum,) = add_product(grad_sum, far, out_weight, [(my_mp ^ bits, 0) for bits in far_bits])
    beside, grad_sum = tie((beside, grad_sum))
    grad_sum = add_product(
        grad_sum, beside, out_weight, [(my_mp ^ bits ^ 1, 0) for bits in far_bits], placing
    )
    grad_places = grad_sum

    weights, lse, seen, mean = local_softmax(query_slots, key_rows, value_rows, entry_lanes)
    grad_slots = exchange(grad_places[0])
    count_lanes = jnp.pad(counts.astype(F32), (0, LANES - blocks_here))
    count_lanes = jnp.broadcast_to(count_lanes[None], (lse.shape[0], LANES))
    all_lse = cube_gather(jnp.concatenate([lse, count_lanes], axis=1)[None], "seq", range(1))
    weights, lse, seen, mean, all_lse, grad_slots = tie(
        (weights, lse, seen, mean, all_lse, grad_slots)
    )
    told = row_dots(n_seq, seen, grad_slots)
    all_told = lax.all_to_all(told, "seq", 0, 0, tiled=True)
    all_lse = cube_gather(all_lse, "seq", range(1, n_seq.bit_length() - 1))
    terms = slope_terms(weights, told, grad_slots, key_rows, value_rows, entry_lanes)
    all_told, all_lse, terms = tie((all_told, all_lse, terms))
    stat, query_terms = query_terms_of(terms, mean, lse, told, all_lse, all_told, partner)
    back = exchange(query_terms).reshape(-1, BLOCK, head_cols)
    query_grad = join_places(
        0, 1, back, None, lists, index_arr, n_seq, slot_cap, entries_here, blocks_here
    )
    key_grad, value_grad = entry_grads(
        weights, stat, query_slots, grad_slots, value_rows, entry_lanes
    )
    key_grad = key_grad.reshape(keys.shape)
    value_grad = value_grad.reshape(values.shape)
    return (query_grad, key_grad, value_grad)


def solution(mesh):
    return jax.shard_map(
        on_device,
        mesh=mesh,
        in_specs=(
            P("seq", "mp"),
            P("mp", None),
            P("seq", "mp"),
            P("seq", None, "mp"),
            P("seq", None, "mp"),
            P(),
            P("seq"),
        ),
        out_specs=(P("seq", "mp"), P("seq", None, "mp"), P("seq", None, "mp")),
        check_vma=False,
    )
```

```python
import functools
import math

import jax
import jax.numpy as jnp
from jax import lax
from jax.experimental import pallas as pl
from jax.experimental.pallas import tpu as pltpu
from jax.sharding import PartitionSpec as P

HEAD = 128
BLOCK = 64
NEIGH = 2
LANES = 128
HEAD_CHUNKS = 1
STEPS = 2
F32 = jnp.float32
BF16 = jnp.bfloat16


def vmem_params(flops=0, moved=0, mib=48):
    return dict(
        compiler_params=pltpu.CompilerParams(vmem_limit_bytes=mib * 1024 * 1024),
        cost_estimate=pl.CostEstimate(flops=flops, bytes_accessed=moved, transcendentals=0),
    )


def slots_of_places(lists_ref, base, places, entries_here, slot_cap):
    owners = [
        lax.div(lists_ref[place % NEIGH, base + place // NEIGH], entries_here)
        for place in range(places)
    ]
    slots = []
    for place, owner in enumerate(owners):
        rank = 0
        for earlier in owners[:place]:
            rank = rank + jnp.where(earlier == owner, 1, 0)
        slots.append(owner * slot_cap + rank)
    return slots


def place_copies(lists_ref, base, rows_ref, out_refs, zero_ref, sems, places, entries_here, slot_cap):
    slots = out_refs[0].shape[0]
    width = out_refs[0].shape[2]
    if slots > places:
        zero_ref[...] = jnp.zeros_like(zero_ref)
        for chunk, out_ref in enumerate(out_refs):
            blanks = [
                pltpu.make_async_copy(zero_ref, out_ref.at[slot], sems.at[chunk, slot])
                for slot in range(slots)
            ]
            for blank in blanks:
                blank.start()
            for blank in blanks:
                blank.wait()
    slot_list = slots_of_places(lists_ref, base, places, entries_here, slot_cap)
    copies = []
    for chunk, out_ref in enumerate(out_refs):
        for place, slot in enumerate(slot_list):
            start = place // NEIGH * BLOCK
            copies.append(
                pltpu.make_async_copy(
                    rows_ref.at[pl.ds(start, BLOCK), pl.ds(chunk * width, width)],
                    out_ref.at[slot],
                    sems.at[chunk, place],
                )
            )
            copies[-1].start()
    for copy in copies:
        copy.wait()


def place_rows(rows, lists, my_index, n_seq, slot_cap, entries_here):
    tok_rows, cols = rows.shape
    places = tok_rows // BLOCK * NEIGH
    slots = n_seq * slot_cap

    def body(lists_ref, index_ref, rows_ref, out_ref, zero_ref, sems):
        place_copies(
            lists_ref,
            index_ref[0] * (places // NEIGH),
            rows_ref,
            [out_ref],
            zero_ref,
            sems,
            places,
            entries_here,
            slot_cap,
        )

    return pl.pallas_call(
        body,
        out_shape=jax.ShapeDtypeStruct((slots, BLOCK, cols), rows.dtype),
        in_specs=[
            pl.BlockSpec(memory_space=pltpu.SMEM),
            pl.BlockSpec(memory_space=pltpu.SMEM),
            pl.BlockSpec(memory_space=pltpu.VMEM),
        ],
        out_specs=pl.BlockSpec(memory_space=pl.ANY),
        scratch_shapes=[
            pltpu.VMEM((BLOCK, cols), rows.dtype),
            pltpu.SemaphoreType.DMA((1, max(slots, places))),
        ],
        name="place_rows",
        **vmem_params(moved=2 * slots * BLOCK * cols * 2, mib=60),
    )(lists, my_index, rows)


def add_product(total, parts, weight, sources, placing=None):
    tok_rows, width = parts[0].shape
    feats = weight.shape[1] // lax.axis_size("mp")
    unit = math.gcd(width, feats)
    cuts = range(width // unit)
    first_units = [source * (feats // unit) + at // unit for source, at in sources]
    cols = weight.shape[0]
    step_cols = cols // (2 * len(parts)) if len(parts) < 3 else min(256, cols)
    steps = cols // step_cols
    places = tok_rows // BLOCK * NEIGH
    before = [] if total is None else [total]
    if placing is None:
        chunks = 1
    else:
        lists, my_index, n_seq, slot_cap, entries_here, chunks = placing
        slots = n_seq * slot_cap

    def body(source_ref, *refs):
        refs = list(refs)
        place_refs = [refs.pop(0) for _ in range(2)] if placing is not None else None
        before_ref = refs.pop(0) if before else None
        part_refs = [refs.pop(0) for _ in parts]
        weight_refs = [[refs.pop(0) for _ in cuts] for _ in parts]
        out_refs = [refs.pop(0) for _ in range(chunks)]
        step = pl.program_id(0)
        result = before_ref[...] if before else 0.0
        for part_ref, weight_cuts in zip(part_refs, weight_refs):
            for cut, weight_ref in zip(cuts, weight_cuts):
                result = result + lax.dot_general(
                    part_ref[:, cut * unit : (cut + 1) * unit],
                    weight_ref[...],
                    NT,
                    preferred_element_type=F32,
                )
        if placing is None:
            out_refs[0][...] = result
            return
        low_ref, zero_ref, sems = refs
        low_ref[:, pl.ds(pl.multiple_of(step * step_cols, step_cols), step_cols)] = result.astype(
            BF16
        )

        @pl.when(step == steps - 1)
        def _():
            lists_ref, index_ref = place_refs
            place_copies(
                lists_ref,
                index_ref[0] * (places // NEIGH),
                low_ref,
                out_refs,
                zero_ref,
                sems,
                places,
                entries_here,
                slot_cap,
            )

    block = pl.BlockSpec((tok_rows, step_cols), lambda k, s: (0, k))
    in_specs = [block] * len(before)
    in_specs += [pl.BlockSpec((tok_rows, width), lambda k, s: (0, 0))] * len(parts)
    for number in range(len(parts)):
        for cut in cuts:
            in_specs.append(
                pl.BlockSpec((step_cols, unit), lambda k, s, n=number, c=cut: (k, s[n] + c))
            )
    if placing is None:
        out_shape, out_specs = [jax.ShapeDtypeStruct((tok_rows, cols), F32)], [block]
        scratch, extra = [], []
    else:
        chunk_cols = cols // chunks
        out_shape = [jax.ShapeDtypeStruct((slots, BLOCK, chunk_cols), BF16)] * chunks
        out_specs = [pl.BlockSpec(memory_space=pl.ANY)] * chunks
        scratch = [
            pltpu.VMEM((tok_rows, cols), BF16),
            pltpu.VMEM((BLOCK, chunk_cols), BF16),
            pltpu.SemaphoreType.DMA((chunks, max(slots, places))),
        ]
        extra = [lists, my_index]
        in_specs = [pl.BlockSpec(memory_space=pltpu.SMEM)] * 2 + in_specs
    return pl.pallas_call(
        body,
        grid_spec=pltpu.PrefetchScalarGridSpec(
            num_scalar_prefetch=1,
            grid=(steps,),
            in_specs=in_specs,
            out_specs=out_specs,
            scratch_shapes=scratch,
        ),
        out_shape=out_shape,
        name="add_product",
        **vmem_params(moved=1, mib=60),
    )(
        jnp.stack(first_units).astype(jnp.int32),
        *extra,
        *before,
        *parts,
        *[weight] * (len(parts) * len(cuts)),
    )


def join_places(
    chunk, chunks, back, before, lists, my_index, n_seq, slot_cap, entries_here, blocks_here
):
    slots, _, cols = back.shape
    places = blocks_here * NEIGH
    kept = [] if before is None else [before]

    def body(lists_ref, index_ref, back_ref, *refs):
        out_ref = refs[-1]
        base = index_ref[0] * (places // NEIGH)
        slot_list = slots_of_places(lists_ref, base, places, entries_here, slot_cap)
        for block in range(blocks_here):
            total = 0.0
            for slot in slot_list[block * NEIGH : (block + 1) * NEIGH]:
                total = total + back_ref[slot].astype(F32)
            out_ref[block * BLOCK : (block + 1) * BLOCK, :] = total.astype(out_ref.dtype)

    return pl.pallas_call(
        body,
        grid=(1,),
        out_shape=jax.ShapeDtypeStruct((blocks_here * BLOCK, chunks * cols), back.dtype),
        in_specs=[
            pl.BlockSpec(memory_space=pltpu.SMEM),
            pl.BlockSpec(memory_space=pltpu.SMEM),
            pl.BlockSpec((slots, BLOCK, cols), lambda i: (0, 0, 0)),
        ]
        + [pl.BlockSpec(memory_space=pl.ANY)] * len(kept),
        out_specs=pl.BlockSpec((blocks_here * BLOCK, cols), lambda i: (0, chunk)),
        input_output_aliases={3: 0} if kept else {},
        name="join_places",
        **vmem_params(moved=3 * slots * BLOCK * cols),
    )(lists, my_index, back, *kept)


def lane_parts(total):
    width = math.gcd(total, 512)
    return [slice(at, at + width) for at in range(0, total, width)]


def pick_entry(stacked, entry):
    entries = stacked.shape[0] // LANES
    chosen = stacked[:LANES]
    for number in range(1, entries):
        chosen = jnp.where(
            entry == number, stacked[number * LANES : (number + 1) * LANES], chosen
        )
    return chosen


def spread_entry(chosen, entry, entries):
    return jnp.concatenate(
        [jnp.where(entry == number, chosen, 0.0) for number in range(entries)], axis=0
    ).astype(BF16)


NT = (((1,), (1,)), ((), ()))
NN = (((1,), (0,)), ((), ()))
TN = (((0,), (0,)), ((), ()))


def local_softmax(query_rows, keys, values, entry_lanes):
    rows, cols = query_rows.shape
    heads = cols // HEAD
    key_rows = keys.shape[0]
    scale = 1.0 / math.sqrt(HEAD)

    def body(query_ref, key_ref, value_ref, entry_ref, weight_ref, lse_ref, seen_ref, mean_ref):
        head = pl.program_id(0)
        for part in lane_parts(rows):
            entry = entry_ref[:, part]
            scores = lax.dot_general(
                key_ref[...], query_ref[part, :], NT, preferred_element_type=F32
            )
            scores = pick_entry(scores, entry) * scale
            top = jnp.max(scores, axis=0, keepdims=True)
            raised = jnp.exp(scores - top)
            total = jnp.sum(raised, axis=0, keepdims=True)
            weights = raised / total
            weight_ref[0, :, part] = weights
            lse_ref[pl.ds(head, 1), part] = top + jnp.log(total)
            wide = spread_entry(weights, entry, key_rows // LANES)
            seen_ref[part, :] = lax.dot_general(
                wide, value_ref[...], TN, preferred_element_type=F32
            )
            mean_ref[part, :] = lax.dot_general(
                wide, key_ref[...], TN, preferred_element_type=F32
            ).astype(BF16)

    column = pl.BlockSpec((rows, HEAD), lambda h: (0, h))
    entry_column = pl.BlockSpec((key_rows, HEAD), lambda h: (0, h))
    return pl.pallas_call(
        body,
        grid=(heads,),
        out_shape=(
            jax.ShapeDtypeStruct((heads, LANES, rows), F32),
            jax.ShapeDtypeStruct((heads, rows), F32),
            jax.ShapeDtypeStruct((rows, cols), F32),
            jax.ShapeDtypeStruct((rows, cols), BF16),
        ),
        in_specs=[
            pl.BlockSpec((rows, HEAD), lambda h: (0, h)),
            entry_column,
            entry_column,
            pl.BlockSpec((1, rows), lambda h: (0, 0)),
        ],
        out_specs=(
            pl.BlockSpec((1, LANES, rows), lambda h: (h, 0, 0)),
            pl.BlockSpec((heads, rows), lambda h: (0, 0)),
            column,
            column,
        ),
        name="local_softmax",
        **vmem_params(moved=1, mib=60),
    )(query_rows, keys, values, entry_lanes)


def partner_lanes(partner_ref, device_row, all_ref, out_ref, slots):
    heads = out_ref.shape[0]
    lane = lax.broadcasted_iota(jnp.int32, (heads, LANES), 1)
    for group in range(slots // 2):
        halves = []
        for half in range(2):
            slot = group * 2 + half
            device, there = partner_ref[device_row, slot], partner_ref[1, slot]
            start = pl.multiple_of(there // 2 * LANES, LANES)
            tile = all_ref[device, :, pl.ds(start, LANES)]
            turned = pltpu.roll(tile, BLOCK, 1)
            halves.append(jnp.where(there % 2 == half, tile, turned))
        out_ref[:, group * LANES : (group + 1) * LANES] = jnp.where(
            lane < BLOCK, halves[0], halves[1]
        )


def live_lanes(partner_ref, all_ref, out_ref, slots, rows):
    lane = lax.broadcasted_iota(jnp.int32, (1, LANES), 1)
    for group in range(slots // 2):
        own, other = [], []
        for half in range(2):
            slot = group * 2 + half
            reader, place = partner_ref[2, slot], partner_ref[3, slot]
            counts = all_ref[reader, 0:1, rows:]
            count = jnp.sum(
                jnp.where(lane == place // NEIGH, counts, 0.0), axis=1, keepdims=True
            )
            at = (place % NEIGH).astype(F32)
            filled = partner_ref[4, slot] > 0
            own.append(jnp.where((at < count) & filled, 1.0, 0.0))
            other.append(jnp.where(NEIGH - 1 - at < count, 1.0, 0.0))
        part = slice(group * LANES, (group + 1) * LANES)
        out_ref[0:1, part] = jnp.where(lane < BLOCK, own[0], own[1])
        out_ref[1:2, part] = jnp.where(lane < BLOCK, other[0], other[1])


def head_columns(heads, cols):
    row = lax.broadcasted_iota(jnp.int32, (heads, cols), 0)
    column = lax.broadcasted_iota(jnp.int32, (heads, cols), 1)
    return jnp.where(row == column // HEAD, 1.0, 0.0).astype(BF16)


def row_dots(n_seq, seen, grad_rows):
    rows, cols = seen.shape
    heads = cols // HEAD
    step_rows = rows // STEPS
    steps = rows // step_rows

    def body(seen_ref, grad_ref, all_ref, told_ref):
        step = pl.program_id(0)
        terms = grad_ref[...].astype(F32) * seen_ref[...]
        high = terms.astype(BF16)
        low = (terms - high.astype(F32)).astype(BF16)
        of_head = head_columns(heads, cols)
        at = pl.ds(pl.multiple_of(step * step_rows, step_rows), step_rows)
        told_ref[:, at] = sum(
            lax.dot_general(of_head, part, NT, preferred_element_type=F32) for part in (high, low)
        )

        @pl.when(step == steps - 1)
        def _():
            for device in range(n_seq):
                all_ref[device] = told_ref[...]

    return pl.pallas_call(
        body,
        grid=(steps,),
        out_shape=jax.ShapeDtypeStruct((n_seq, heads, rows), F32),
        in_specs=[
            pl.BlockSpec((step_rows, cols), lambda i: (i, 0)),
            pl.BlockSpec((step_rows, cols), lambda i: (i, 0)),
        ],
        out_specs=pl.BlockSpec((n_seq, heads, rows), lambda i: (0, 0, 0)),
        scratch_shapes=[pltpu.VMEM((heads, rows), F32)],
        name="row_dots",
        **vmem_params(moved=1, mib=60),
    )(seen, grad_rows)


def slope_terms(weights, told, grad_rows, keys, values, entry_lanes):
    heads, _, rows = weights.shape
    cols = heads * HEAD
    key_rows = keys.shape[0]

    def body(weight_ref, told_ref, grad_ref, key_ref, value_ref, entry_ref, out_ref):
        head = pl.program_id(0)
        for part in lane_parts(rows):
            entry = entry_ref[:, part]
            slope = lax.dot_general(
                value_ref[...], grad_ref[part, :], NT, preferred_element_type=F32
            )
            dot = told_ref[0, pl.ds(head, 1), part]
            terms = weight_ref[0, :, part] * (pick_entry(slope, entry) - dot)
            wide = spread_entry(terms, entry, key_rows // LANES)
            out_ref[part, :] = lax.dot_general(
                wide, key_ref[...], TN, preferred_element_type=F32
            ).astype(BF16)

    column = pl.BlockSpec((rows, HEAD), lambda h: (0, h))
    entry_column = pl.BlockSpec((key_rows, HEAD), lambda h: (0, h))
    return pl.pallas_call(
        body,
        grid=(heads,),
        out_shape=jax.ShapeDtypeStruct((rows, cols), BF16),
        in_specs=[
            pl.BlockSpec((1, LANES, rows), lambda h: (h, 0, 0)),
            pl.BlockSpec((1,) + told.shape[1:], lambda h: (0, 0, 0)),
            pl.BlockSpec((rows, HEAD), lambda h: (0, h)),
            entry_column,
            entry_column,
            pl.BlockSpec((1, rows), lambda h: (0, 0)),
        ],
        out_specs=column,
        name="slope_terms",
        **vmem_params(moved=1, mib=60),
    )(weights, told, grad_rows, keys, values, entry_lanes)


def query_terms_of(terms, mean, lse, dots, all_lse, all_dots, partner):
    rows, cols = terms.shape
    heads = cols // HEAD
    slots = rows // BLOCK
    step_rows = rows // STEPS
    scale = 1.0 / math.sqrt(HEAD)

    def body(partner_ref, lse_ref, dot_ref, all_lse_ref, all_dot_ref, term_ref, mean_ref, *refs):
        stat_ref, out_ref, other_ref, apart_ref, live_ref, more_ref = refs
        step = pl.program_id(0)

        @pl.when(step == 0)
        def _():
            partner_lanes(partner_ref, 5, all_lse_ref, apart_ref, slots)
            partner_lanes(partner_ref, 0, all_dot_ref, other_ref, slots)
            live_lanes(partner_ref, all_lse_ref, live_ref, slots, rows)
            own = dot_ref[0]
            apart = apart_ref[...] - lse_ref[...]
            own_live, other_live = live_ref[0:1, :] > 0.0, live_ref[1:2, :] > 0.0
            odds = jnp.where(other_live, jnp.exp(apart), 0.0)
            share = jnp.where(own_live, 1.0 / (1.0 + odds), 0.0)
            rest = jnp.where(other_live, 1.0 / (1.0 + jnp.exp(-apart)), 0.0)
            more = rest * (other_ref[...] - own)
            stat_ref[:heads, :] = share
            stat_ref[heads:, :] = own + more
            more_ref[...] = more

        at = pl.ds(pl.multiple_of(step * step_rows, step_rows), step_rows)
        of_head = jnp.concatenate([head_columns(heads, cols)] * 2, axis=0)

        def spread(rows_of_heads):
            high = rows_of_heads.astype(BF16)
            low = (rows_of_heads - high.astype(F32)).astype(BF16)
            return lax.dot_general(
                jnp.concatenate([high, low], axis=0), of_head, TN, preferred_element_type=F32
            )

        share, more = spread(stat_ref[:heads, at]), spread(more_ref[:, at])
        query = share * (term_ref[...].astype(F32) - more * mean_ref[...].astype(F32))
        out_ref[...] = (query * scale).astype(BF16)

    block = pl.BlockSpec((step_rows, cols), lambda i: (i, 0))
    return pl.pallas_call(
        body,
        grid=(rows // step_rows,),
        out_shape=(
            jax.ShapeDtypeStruct((2 * heads, rows), F32),
            jax.ShapeDtypeStruct((rows, cols), BF16),
        ),
        in_specs=[
            pl.BlockSpec(memory_space=pltpu.SMEM),
            pl.BlockSpec((heads, rows), lambda i: (0, 0)),
            pl.BlockSpec((1, heads, rows), lambda i: (0, 0, 0)),
            pl.BlockSpec(all_lse.shape, lambda i: (0, 0, 0)),
            pl.BlockSpec(all_dots.shape, lambda i: (0, 0, 0)),
            pl.BlockSpec((step_rows, cols), lambda i: (i, 0)),
            pl.BlockSpec((step_rows, cols), lambda i: (i, 0)),
        ],
        out_specs=(pl.BlockSpec((2 * heads, rows), lambda i: (0, 0)), block),
        scratch_shapes=[
            pltpu.VMEM((heads, rows), F32),
            pltpu.VMEM((heads, rows), F32),
            pltpu.VMEM((2, rows), F32),
            pltpu.VMEM((heads, rows), F32),
        ],
        name="query_terms",
        **vmem_params(moved=1, mib=60),
    )(partner, lse, dots, all_lse, all_dots, terms, mean)


def entry_grads(weights, stat, query_rows, grad_rows, values, entry_lanes):
    heads, _, rows = weights.shape
    cols = heads * HEAD
    entry_rows = values.shape[0]
    scale = 1.0 / math.sqrt(HEAD)

    def body(weight_ref, stat_ref, query_ref, grad_ref, value_ref, entry_ref, key_out, value_out):
        head = pl.program_id(0)
        key_sum = jnp.zeros((entry_rows, HEAD), F32)
        value_sum = jnp.zeros((entry_rows, HEAD), F32)
        for part in lane_parts(rows):
            entry = entry_ref[:, part]
            grad = grad_ref[part, :]
            joint = weight_ref[0, :, part] * stat_ref[pl.ds(head, 1), part]
            slope = lax.dot_general(value_ref[...], grad, NT, preferred_element_type=F32)
            low = joint * (pick_entry(slope, entry) - stat_ref[pl.ds(heads + head, 1), part])
            wide = spread_entry(joint, entry, entry_rows // LANES)
            value_sum += lax.dot_general(wide, grad, NN, preferred_element_type=F32)
            wide = spread_entry(low, entry, entry_rows // LANES)
            key_sum += lax.dot_general(wide, query_ref[part, :], NN, preferred_element_type=F32)
        key_out[...] = (key_sum * scale).astype(BF16)
        value_out[...] = value_sum.astype(BF16)

    entry_column = pl.BlockSpec((entry_rows, HEAD), lambda h: (0, h))
    return pl.pallas_call(
        body,
        grid=(heads,),
        out_shape=[jax.ShapeDtypeStruct((entry_rows, cols), BF16)] * 2,
        in_specs=[
            pl.BlockSpec((1, LANES, rows), lambda h: (h, 0, 0)),
            pl.BlockSpec((2 * heads, rows), lambda h: (0, 0)),
            pl.BlockSpec((rows, HEAD), lambda h: (0, h)),
            pl.BlockSpec((rows, HEAD), lambda h: (0, h)),
            pl.BlockSpec((entry_rows, HEAD), lambda h: (0, h)),
            pl.BlockSpec((1, rows), lambda h: (0, 0)),
        ],
        out_specs=[entry_column] * 2,
        name="entry_grads",
        **vmem_params(moved=1, mib=60),
    )(weights, stat, query_rows, grad_rows, values, entry_lanes)


def swap(value, axis, bits):
    size = lax.axis_size(axis)
    return lax.ppermute(value, axis, [(i, i ^ bits) for i in range(size)])


def cube_gather(value, axis, steps):
    for step in steps:
        bits = lax.axis_size(axis) >> (step + 1)
        value = jnp.concatenate([value, swap(value, axis, bits)], axis=0)
    return value


def rank_slots(owners):
    slot_total = owners.shape[-1]
    earlier_mask = jnp.arange(slot_total)[None, :] < jnp.arange(slot_total)[:, None]
    same_owner = owners[..., :, None] == owners[..., None, :]
    return jnp.sum(same_owner & earlier_mask, axis=-1)


def owner_tables(all_lists, my_index, entries_here, slot_cap):
    n_seq, places = all_lists.shape
    owners = all_lists // entries_here
    ranks = rank_slots(owners)
    chosen = (owners == my_index)[:, None, :] & (
        ranks[:, None, :] == jnp.arange(slot_cap)[None, :, None]
    )

    def look(table):
        return jnp.sum(jnp.where(chosen, table[:, None, :], 0), axis=2).reshape(-1)

    def other(table):
        return table.reshape(n_seq, -1, NEIGH)[:, :, ::-1].reshape(n_seq, places)

    reader = jnp.arange(n_seq)[:, None]

    def turned(device):
        apart, position, bits = device ^ my_index, 0, n_seq >> 1
        for step in range(n_seq.bit_length() - 1):
            position = position + (apart >> step) % 2 * (bits >> step)
        return position

    partner = [
        look(other(owners)),
        look(other(ranks) + slot_cap * reader),
        look(turned(reader) + jnp.zeros_like(owners)),
        look(jnp.arange(places) + jnp.zeros_like(owners)),
        look(jnp.ones_like(owners)),
        look(turned(other(owners))),
    ]
    entry = look(all_lists % entries_here)
    return (
        jnp.repeat(entry[None], BLOCK, axis=1).astype(jnp.int32),
        jnp.stack(partner).astype(jnp.int32),
    )


def on_device(out_grad, out_weight, queries, keys, values, retrieval, counts):
    n_seq, n_mp = lax.axis_size("seq"), lax.axis_size("mp")
    my_index, my_mp = lax.axis_index("seq"), lax.axis_index("mp")
    tok_rows, head_cols = queries.shape
    entries_here, nbr_rows, _ = keys.shape
    blocks_here = tok_rows // BLOCK
    places = blocks_here * NEIGH
    slot_cap = (places + n_seq - 1) // n_seq
    rows = n_seq * slot_cap * BLOCK
    feats = out_grad.shape[1]
    lists = retrieval.T
    index_arr = my_index.astype(jnp.int32).reshape(1)
    key_rows = keys.reshape(entries_here * nbr_rows, head_cols)
    value_rows = values.reshape(entries_here * nbr_rows, head_cols)

    def exchange(slot_rows):
        cols = slot_rows.shape[-1]
        return lax.all_to_all(
            slot_rows.reshape(n_seq, slot_cap * BLOCK, cols), "seq", 0, 0, tiled=True
        ).reshape(rows, cols)

    far_bits = list(range(2, n_mp, 2))
    tie = lax.optimization_barrier
    far = [swap(out_grad, "mp", bits) for bits in far_bits]
    near = swap(out_grad, "mp", 1)
    query_places = place_rows(queries, lists, index_arr, n_seq, slot_cap, entries_here)
    query_slots = exchange(query_places)
    entry_lanes, partner = owner_tables(
        retrieval.reshape(n_seq, places), my_index, entries_here, slot_cap
    )

    placing = (lists, index_arr, n_seq, slot_cap, entries_here, HEAD_CHUNKS)
    (grad_sum,) = add_product(None, [out_grad, near], out_weight, [(my_mp, 0), (my_mp ^ 1, 0)])
    far, grad_sum = tie((far, grad_sum))
    beside = [swap(part, "mp", 1) for part in far]
    (grad_sum,) = add_product(grad_sum, far, out_weight, [(my_mp ^ bits, 0) for bits in far_bits])
    beside, grad_sum = tie((beside, grad_sum))
    grad_sum = add_product(
        grad_sum, beside, out_weight, [(my_mp ^ bits ^ 1, 0) for bits in far_bits], placing
    )
    grad_places = grad_sum

    weights, lse, seen, mean = local_softmax(query_slots, key_rows, value_rows, entry_lanes)
    grad_slots = exchange(grad_places[0])
    count_lanes = jnp.pad(counts.astype(F32), (0, LANES - blocks_here))
    count_lanes = jnp.broadcast_to(count_lanes[None], (lse.shape[0], LANES))
    all_lse = cube_gather(jnp.concatenate([lse, count_lanes], axis=1)[None], "seq", range(1))
    weights, lse, seen, mean, all_lse, partner, grad_slots = tie(
        (weights, lse, seen, mean, all_lse, partner, grad_slots)
    )
    told = row_dots(n_seq, seen, grad_slots)
    all_told = lax.all_to_all(told, "seq", 0, 0, tiled=True)
    all_lse = cube_gather(all_lse, "seq", range(1, n_seq.bit_length() - 1))
    terms = slope_terms(weights, told, grad_slots, key_rows, value_rows, entry_lanes)
    all_told, all_lse, terms = tie((all_told, all_lse, terms))
    stat, query_terms = query_terms_of(terms, mean, lse, told, all_lse, all_told, partner)
    back = exchange(query_terms).reshape(-1, BLOCK, head_cols)
    query_grad = join_places(
        0, 1, back, None, lists, index_arr, n_seq, slot_cap, entries_here, blocks_here
    )
    key_grad, value_grad = entry_grads(
        weights, stat, query_slots, grad_slots, value_rows, entry_lanes
    )
    key_grad = key_grad.reshape(keys.shape)
    value_grad = value_grad.reshape(values.shape)
    return (query_grad, key_grad, value_grad)


def solution(mesh):
    return jax.shard_map(
        on_device,
        mesh=mesh,
        in_specs=(
            P("seq", "mp"),
            P("mp", None),
            P("seq", "mp"),
            P("seq", None, "mp"),
            P("seq", None, "mp"),
            P(),
            P("seq"),
        ),
        out_specs=(P("seq", "mp"), P("seq", None, "mp"), P("seq", None, "mp")),
        check_vma=False,
    )
```

```python
import functools
import math

import jax
import jax.numpy as jnp
from jax import lax
from jax.experimental import pallas as pl
from jax.experimental.pallas import tpu as pltpu
from jax.sharding import PartitionSpec as P

HEAD = 128
BLOCK = 64
NEIGH = 2
LANES = 128
HEAD_CHUNKS = 1
STEPS = 2
F32 = jnp.float32
BF16 = jnp.bfloat16


def vmem_params(flops=0, moved=0, mib=48):
    return dict(
        compiler_params=pltpu.CompilerParams(vmem_limit_bytes=mib * 1024 * 1024),
        cost_estimate=pl.CostEstimate(flops=flops, bytes_accessed=moved, transcendentals=0),
    )


def slots_of_places(lists_ref, base, places, entries_here, slot_cap):
    owners = [
        lax.div(lists_ref[place % NEIGH, base + place // NEIGH], entries_here)
        for place in range(places)
    ]
    slots = []
    for place, owner in enumerate(owners):
        rank = 0
        for earlier in owners[:place]:
            rank = rank + jnp.where(earlier == owner, 1, 0)
        slots.append(owner * slot_cap + rank)
    return slots


def place_copies(lists_ref, base, rows_ref, out_refs, zero_ref, sems, places, entries_here, slot_cap):
    slots = out_refs[0].shape[0]
    width = out_refs[0].shape[2]
    if slots > places:
        zero_ref[...] = jnp.zeros_like(zero_ref)
        for chunk, out_ref in enumerate(out_refs):
            blanks = [
                pltpu.make_async_copy(zero_ref, out_ref.at[slot], sems.at[chunk, slot])
                for slot in range(slots)
            ]
            for blank in blanks:
                blank.start()
            for blank in blanks:
                blank.wait()
    slot_list = slots_of_places(lists_ref, base, places, entries_here, slot_cap)
    copies = []
    for chunk, out_ref in enumerate(out_refs):
        for place, slot in enumerate(slot_list):
            start = place // NEIGH * BLOCK
            copies.append(
                pltpu.make_async_copy(
                    rows_ref.at[pl.ds(start, BLOCK), pl.ds(chunk * width, width)],
                    out_ref.at[slot],
                    sems.at[chunk, place],
                )
            )
            copies[-1].start()
    for copy in copies:
        copy.wait()


def place_rows(rows, lists, my_index, n_seq, slot_cap, entries_here):
    tok_rows, cols = rows.shape
    places = tok_rows // BLOCK * NEIGH
    slots = n_seq * slot_cap

    def body(lists_ref, index_ref, rows_ref, out_ref, zero_ref, sems):
        place_copies(
            lists_ref,
            index_ref[0] * (places // NEIGH),
            rows_ref,
            [out_ref],
            zero_ref,
            sems,
            places,
            entries_here,
            slot_cap,
        )

    return pl.pallas_call(
        body,
        out_shape=jax.ShapeDtypeStruct((slots, BLOCK, cols), rows.dtype),
        in_specs=[
            pl.BlockSpec(memory_space=pltpu.SMEM),
            pl.BlockSpec(memory_space=pltpu.SMEM),
            pl.BlockSpec(memory_space=pltpu.VMEM),
        ],
        out_specs=pl.BlockSpec(memory_space=pl.ANY),
        scratch_shapes=[
            pltpu.VMEM((BLOCK, cols), rows.dtype),
            pltpu.SemaphoreType.DMA((1, max(slots, places))),
        ],
        name="place_rows",
        **vmem_params(moved=2 * slots * BLOCK * cols * 2, mib=60),
    )(lists, my_index, rows)


def add_product(total, parts, weight, sources, placing=None):
    tok_rows, width = parts[0].shape
    feats = weight.shape[1] // lax.axis_size("mp")
    unit = math.gcd(width, feats)
    cuts = range(width // unit)
    first_units = [source * (feats // unit) + at // unit for source, at in sources]
    cols = weight.shape[0]
    step_cols = cols // (2 * len(parts)) if len(parts) < 3 else min(256, cols)
    steps = cols // step_cols
    places = tok_rows // BLOCK * NEIGH
    before = [] if total is None else [total]
    if placing is None:
        chunks = 1
    else:
        lists, my_index, n_seq, slot_cap, entries_here, chunks = placing
        slots = n_seq * slot_cap

    def body(source_ref, *refs):
        refs = list(refs)
        place_refs = [refs.pop(0) for _ in range(2)] if placing is not None else None
        before_ref = refs.pop(0) if before else None
        part_refs = [refs.pop(0) for _ in parts]
        weight_refs = [[refs.pop(0) for _ in cuts] for _ in parts]
        out_refs = [refs.pop(0) for _ in range(chunks)]
        step = pl.program_id(0)
        result = before_ref[...] if before else 0.0
        for part_ref, weight_cuts in zip(part_refs, weight_refs):
            for cut, weight_ref in zip(cuts, weight_cuts):
                result = result + lax.dot_general(
                    part_ref[:, cut * unit : (cut + 1) * unit],
                    weight_ref[...],
                    NT,
                    preferred_element_type=F32,
                )
        if placing is None:
            out_refs[0][...] = result
            return
        low_ref, zero_ref, sems = refs
        low_ref[:, pl.ds(pl.multiple_of(step * step_cols, step_cols), step_cols)] = result.astype(
            BF16
        )

        @pl.when(step == steps - 1)
        def _():
            lists_ref, index_ref = place_refs
            place_copies(
                lists_ref,
                index_ref[0] * (places // NEIGH),
                low_ref,
                out_refs,
                zero_ref,
                sems,
                places,
                entries_here,
                slot_cap,
            )

    block = pl.BlockSpec((tok_rows, step_cols), lambda k, s: (0, k))
    in_specs = [block] * len(before)
    in_specs += [pl.BlockSpec((tok_rows, width), lambda k, s: (0, 0))] * len(parts)
    for number in range(len(parts)):
        for cut in cuts:
            in_specs.append(
                pl.BlockSpec((step_cols, unit), lambda k, s, n=number, c=cut: (k, s[n] + c))
            )
    if placing is None:
        out_shape, out_specs = [jax.ShapeDtypeStruct((tok_rows, cols), F32)], [block]
        scratch, extra = [], []
    else:
        chunk_cols = cols // chunks
        out_shape = [jax.ShapeDtypeStruct((slots, BLOCK, chunk_cols), BF16)] * chunks
        out_specs = [pl.BlockSpec(memory_space=pl.ANY)] * chunks
        scratch = [
            pltpu.VMEM((tok_rows, cols), BF16),
            pltpu.VMEM((BLOCK, chunk_cols), BF16),
            pltpu.SemaphoreType.DMA((chunks, max(slots, places))),
        ]
        extra = [lists, my_index]
        in_specs = [pl.BlockSpec(memory_space=pltpu.SMEM)] * 2 + in_specs
    return pl.pallas_call(
        body,
        grid_spec=pltpu.PrefetchScalarGridSpec(
            num_scalar_prefetch=1,
            grid=(steps,),
            in_specs=in_specs,
            out_specs=out_specs,
            scratch_shapes=scratch,
        ),
        out_shape=out_shape,
        name="add_product",
        **vmem_params(moved=1, mib=60),
    )(
        jnp.stack(first_units).astype(jnp.int32),
        *extra,
        *before,
        *parts,
        *[weight] * (len(parts) * len(cuts)),
    )


def join_places(
    chunk, chunks, back, before, lists, my_index, n_seq, slot_cap, entries_here, blocks_here
):
    slots, _, cols = back.shape
    places = blocks_here * NEIGH
    kept = [] if before is None else [before]

    def body(lists_ref, index_ref, back_ref, *refs):
        out_ref = refs[-1]
        base = index_ref[0] * (places // NEIGH)
        slot_list = slots_of_places(lists_ref, base, places, entries_here, slot_cap)
        for block in range(blocks_here):
            total = 0.0
            for slot in slot_list[block * NEIGH : (block + 1) * NEIGH]:
                total = total + back_ref[slot].astype(F32)
            out_ref[block * BLOCK : (block + 1) * BLOCK, :] = total.astype(out_ref.dtype)

    return pl.pallas_call(
        body,
        grid=(1,),
        out_shape=jax.ShapeDtypeStruct((blocks_here * BLOCK, chunks * cols), back.dtype),
        in_specs=[
            pl.BlockSpec(memory_space=pltpu.SMEM),
            pl.BlockSpec(memory_space=pltpu.SMEM),
            pl.BlockSpec((slots, BLOCK, cols), lambda i: (0, 0, 0)),
        ]
        + [pl.BlockSpec(memory_space=pl.ANY)] * len(kept),
        out_specs=pl.BlockSpec((blocks_here * BLOCK, cols), lambda i: (0, chunk)),
        input_output_aliases={3: 0} if kept else {},
        name="join_places",
        **vmem_params(moved=3 * slots * BLOCK * cols),
    )(lists, my_index, back, *kept)


def lane_parts(total):
    width = math.gcd(total, 512)
    return [slice(at, at + width) for at in range(0, total, width)]


def pick_entry(stacked, entry):
    entries = stacked.shape[0] // LANES
    chosen = stacked[:LANES]
    for number in range(1, entries):
        chosen = jnp.where(
            entry == number, stacked[number * LANES : (number + 1) * LANES], chosen
        )
    return chosen


def spread_entry(chosen, entry, entries):
    return jnp.concatenate(
        [jnp.where(entry == number, chosen, 0.0) for number in range(entries)], axis=0
    ).astype(BF16)


NT = (((1,), (1,)), ((), ()))
NN = (((1,), (0,)), ((), ()))
TN = (((0,), (0,)), ((), ()))


def local_softmax(query_rows, keys, values, entry_lanes):
    rows, cols = query_rows.shape
    heads = cols // HEAD
    key_rows = keys.shape[0]
    scale = 1.0 / math.sqrt(HEAD)

    def body(query_ref, key_ref, value_ref, entry_ref, weight_ref, lse_ref, seen_ref, mean_ref):
        head = pl.program_id(0)
        for part in lane_parts(rows):
            entry = entry_ref[:, part]
            scores = lax.dot_general(
                key_ref[...], query_ref[part, :], NT, preferred_element_type=F32
            )
            scores = pick_entry(scores, entry) * scale
            top = jnp.max(scores, axis=0, keepdims=True)
            raised = jnp.exp(scores - top)
            total = jnp.sum(raised, axis=0, keepdims=True)
            weights = raised / total
            weight_ref[0, :, part] = weights
            lse_ref[pl.ds(head, 1), part] = top + jnp.log(total)
            wide = spread_entry(weights, entry, key_rows // LANES)
            seen_ref[part, :] = lax.dot_general(
                wide, value_ref[...], TN, preferred_element_type=F32
            )
            mean_ref[part, :] = lax.dot_general(
                wide, key_ref[...], TN, preferred_element_type=F32
            ).astype(BF16)

    column = pl.BlockSpec((rows, HEAD), lambda h: (0, h))
    entry_column = pl.BlockSpec((key_rows, HEAD), lambda h: (0, h))
    return pl.pallas_call(
        body,
        grid=(heads,),
        out_shape=(
            jax.ShapeDtypeStruct((heads, LANES, rows), F32),
            jax.ShapeDtypeStruct((heads, rows), F32),
            jax.ShapeDtypeStruct((rows, cols), F32),
            jax.ShapeDtypeStruct((rows, cols), BF16),
        ),
        in_specs=[
            pl.BlockSpec((rows, HEAD), lambda h: (0, h)),
            entry_column,
            entry_column,
            pl.BlockSpec((1, rows), lambda h: (0, 0)),
        ],
        out_specs=(
            pl.BlockSpec((1, LANES, rows), lambda h: (h, 0, 0)),
            pl.BlockSpec((heads, rows), lambda h: (0, 0)),
            column,
            column,
        ),
        name="local_softmax",
        **vmem_params(moved=1, mib=60),
    )(query_rows, keys, values, entry_lanes)


def partner_lanes(partner_ref, device_row, all_ref, out_ref, slots):
    heads = out_ref.shape[0]
    lane = lax.broadcasted_iota(jnp.int32, (heads, LANES), 1)
    for group in range(slots // 2):
        halves = []
        for half in range(2):
            slot = group * 2 + half
            device, there = partner_ref[device_row, slot], partner_ref[1, slot]
            start = pl.multiple_of(there // 2 * LANES, LANES)
            tile = all_ref[device, :, pl.ds(start, LANES)]
            turned = pltpu.roll(tile, BLOCK, 1)
            halves.append(jnp.where(there % 2 == half, tile, turned))
        out_ref[:, group * LANES : (group + 1) * LANES] = jnp.where(
            lane < BLOCK, halves[0], halves[1]
        )


def live_lanes(partner_ref, all_ref, out_ref, slots, rows):
    lane = lax.broadcasted_iota(jnp.int32, (1, LANES), 1)
    for group in range(slots // 2):
        own, other = [], []
        for half in range(2):
            slot = group * 2 + half
            reader, place = partner_ref[2, slot], partner_ref[3, slot]
            counts = all_ref[reader, 0:1, rows:]
            count = jnp.sum(
                jnp.where(lane == place // NEIGH, counts, 0.0), axis=1, keepdims=True
            )
            at = (place % NEIGH).astype(F32)
            filled = partner_ref[4, slot] > 0
            own.append(jnp.where((at < count) & filled, 1.0, 0.0))
            other.append(jnp.where(NEIGH - 1 - at < count, 1.0, 0.0))
        part = slice(group * LANES, (group + 1) * LANES)
        out_ref[0:1, part] = jnp.where(lane < BLOCK, own[0], own[1])
        out_ref[1:2, part] = jnp.where(lane < BLOCK, other[0], other[1])


def head_columns(heads, cols):
    row = lax.broadcasted_iota(jnp.int32, (heads, cols), 0)
    column = lax.broadcasted_iota(jnp.int32, (heads, cols), 1)
    return jnp.where(row == column // HEAD, 1.0, 0.0).astype(BF16)


def row_dots(n_seq, seen, grad_rows):
    rows, cols = seen.shape
    heads = cols // HEAD
    step_rows = rows // STEPS
    steps = rows // step_rows

    def body(seen_ref, grad_ref, all_ref, told_ref):
        step = pl.program_id(0)
        terms = grad_ref[...].astype(F32) * seen_ref[...]
        high = terms.astype(BF16)
        low = (terms - high.astype(F32)).astype(BF16)
        of_head = head_columns(heads, cols)
        at = pl.ds(pl.multiple_of(step * step_rows, step_rows), step_rows)
        told_ref[:, at] = sum(
            lax.dot_general(of_head, part, NT, preferred_element_type=F32) for part in (high, low)
        )

        @pl.when(step == steps - 1)
        def _():
            for device in range(n_seq):
                all_ref[device] = told_ref[...]

    return pl.pallas_call(
        body,
        grid=(steps,),
        out_shape=jax.ShapeDtypeStruct((n_seq, heads, rows), F32),
        in_specs=[
            pl.BlockSpec((step_rows, cols), lambda i: (i, 0)),
            pl.BlockSpec((step_rows, cols), lambda i: (i, 0)),
        ],
        out_specs=pl.BlockSpec((n_seq, heads, rows), lambda i: (0, 0, 0)),
        scratch_shapes=[pltpu.VMEM((heads, rows), F32)],
        name="row_dots",
        **vmem_params(moved=1, mib=32),
    )(seen, grad_rows)


def slope_terms(weights, told, grad_rows, keys, values, entry_lanes):
    heads, _, rows = weights.shape
    cols = heads * HEAD
    key_rows = keys.shape[0]

    def body(weight_ref, told_ref, grad_ref, key_ref, value_ref, entry_ref, out_ref):
        head = pl.program_id(0)
        for part in lane_parts(rows):
            entry = entry_ref[:, part]
            slope = lax.dot_general(
                value_ref[...], grad_ref[part, :], NT, preferred_element_type=F32
            )
            dot = told_ref[0, pl.ds(head, 1), part]
            terms = weight_ref[0, :, part] * (pick_entry(slope, entry) - dot)
            wide = spread_entry(terms, entry, key_rows // LANES)
            out_ref[part, :] = lax.dot_general(
                wide, key_ref[...], TN, preferred_element_type=F32
            ).astype(BF16)

    column = pl.BlockSpec((rows, HEAD), lambda h: (0, h))
    entry_column = pl.BlockSpec((key_rows, HEAD), lambda h: (0, h))
    return pl.pallas_call(
        body,
        grid=(heads,),
        out_shape=jax.ShapeDtypeStruct((rows, cols), BF16),
        in_specs=[
            pl.BlockSpec((1, LANES, rows), lambda h: (h, 0, 0)),
            pl.BlockSpec((1,) + told.shape[1:], lambda h: (0, 0, 0)),
            pl.BlockSpec((rows, HEAD), lambda h: (0, h)),
            entry_column,
            entry_column,
            pl.BlockSpec((1, rows), lambda h: (0, 0)),
        ],
        out_specs=column,
        name="slope_terms",
        **vmem_params(moved=1, mib=60),
    )(weights, told, grad_rows, keys, values, entry_lanes)


def query_terms_of(terms, mean, lse, dots, all_lse, all_dots, partner):
    rows, cols = terms.shape
    heads = cols // HEAD
    slots = rows // BLOCK
    step_rows = rows // STEPS
    scale = 1.0 / math.sqrt(HEAD)

    def body(partner_ref, lse_ref, dot_ref, all_lse_ref, all_dot_ref, term_ref, mean_ref, *refs):
        stat_ref, out_ref, other_ref, apart_ref, live_ref, more_ref = refs
        step = pl.program_id(0)

        @pl.when(step == 0)
        def _():
            partner_lanes(partner_ref, 5, all_lse_ref, apart_ref, slots)
            partner_lanes(partner_ref, 0, all_dot_ref, other_ref, slots)
            live_lanes(partner_ref, all_lse_ref, live_ref, slots, rows)
            own = dot_ref[0]
            apart = apart_ref[...] - lse_ref[...]
            own_live, other_live = live_ref[0:1, :] > 0.0, live_ref[1:2, :] > 0.0
            odds = jnp.where(other_live, jnp.exp(apart), 0.0)
            share = jnp.where(own_live, 1.0 / (1.0 + odds), 0.0)
            rest = jnp.where(other_live, 1.0 / (1.0 + jnp.exp(-apart)), 0.0)
            more = rest * (other_ref[...] - own)
            stat_ref[:heads, :] = share
            stat_ref[heads:, :] = own + more
            more_ref[...] = more

        at = pl.ds(pl.multiple_of(step * step_rows, step_rows), step_rows)
        of_head = jnp.concatenate([head_columns(heads, cols)] * 2, axis=0)

        def spread(rows_of_heads):
            high = rows_of_heads.astype(BF16)
            low = (rows_of_heads - high.astype(F32)).astype(BF16)
            return lax.dot_general(
                jnp.concatenate([high, low], axis=0), of_head, TN, preferred_element_type=F32
            )

        share, more = spread(stat_ref[:heads, at]), spread(more_ref[:, at])
        query = share * (term_ref[...].astype(F32) - more * mean_ref[...].astype(F32))
        out_ref[...] = (query * scale).astype(BF16)

    block = pl.BlockSpec((step_rows, cols), lambda i: (i, 0))
    return pl.pallas_call(
        body,
        grid=(rows // step_rows,),
        out_shape=(
            jax.ShapeDtypeStruct((2 * heads, rows), F32),
            jax.ShapeDtypeStruct((rows, cols), BF16),
        ),
        in_specs=[
            pl.BlockSpec(memory_space=pltpu.SMEM),
            pl.BlockSpec((heads, rows), lambda i: (0, 0)),
            pl.BlockSpec((1, heads, rows), lambda i: (0, 0, 0)),
            pl.BlockSpec(all_lse.shape, lambda i: (0, 0, 0)),
            pl.BlockSpec(all_dots.shape, lambda i: (0, 0, 0)),
            pl.BlockSpec((step_rows, cols), lambda i: (i, 0)),
            pl.BlockSpec((step_rows, cols), lambda i: (i, 0)),
        ],
        out_specs=(pl.BlockSpec((2 * heads, rows), lambda i: (0, 0)), block),
        scratch_shapes=[
            pltpu.VMEM((heads, rows), F32),
            pltpu.VMEM((heads, rows), F32),
            pltpu.VMEM((2, rows), F32),
            pltpu.VMEM((heads, rows), F32),
        ],
        name="query_terms",
        **vmem_params(moved=1, mib=60),
    )(partner, lse, dots, all_lse, all_dots, terms, mean)


def entry_grads(weights, stat, query_rows, grad_rows, values, entry_lanes):
    heads, _, rows = weights.shape
    cols = heads * HEAD
    entry_rows = values.shape[0]
    scale = 1.0 / math.sqrt(HEAD)

    def body(weight_ref, stat_ref, query_ref, grad_ref, value_ref, entry_ref, key_out, value_out):
        head = pl.program_id(0)
        key_sum = jnp.zeros((entry_rows, HEAD), F32)
        value_sum = jnp.zeros((entry_rows, HEAD), F32)
        for part in lane_parts(rows):
            entry = entry_ref[:, part]
            grad = grad_ref[part, :]
            joint = weight_ref[0, :, part] * stat_ref[pl.ds(head, 1), part]
            slope = lax.dot_general(value_ref[...], grad, NT, preferred_element_type=F32)
            low = joint * (pick_entry(slope, entry) - stat_ref[pl.ds(heads + head, 1), part])
            wide = spread_entry(joint, entry, entry_rows // LANES)
            value_sum += lax.dot_general(wide, grad, NN, preferred_element_type=F32)
            wide = spread_entry(low, entry, entry_rows // LANES)
            key_sum += lax.dot_general(wide, query_ref[part, :], NN, preferred_element_type=F32)
        key_out[...] = (key_sum * scale).astype(BF16)
        value_out[...] = value_sum.astype(BF16)

    entry_column = pl.BlockSpec((entry_rows, HEAD), lambda h: (0, h))
    return pl.pallas_call(
        body,
        grid=(heads,),
        out_shape=[jax.ShapeDtypeStruct((entry_rows, cols), BF16)] * 2,
        in_specs=[
            pl.BlockSpec((1, LANES, rows), lambda h: (h, 0, 0)),
            pl.BlockSpec((2 * heads, rows), lambda h: (0, 0)),
            pl.BlockSpec((rows, HEAD), lambda h: (0, h)),
            pl.BlockSpec((rows, HEAD), lambda h: (0, h)),
            pl.BlockSpec((entry_rows, HEAD), lambda h: (0, h)),
            pl.BlockSpec((1, rows), lambda h: (0, 0)),
        ],
        out_specs=[entry_column] * 2,
        name="entry_grads",
        **vmem_params(moved=1, mib=60),
    )(weights, stat, query_rows, grad_rows, values, entry_lanes)


def swap(value, axis, bits):
    size = lax.axis_size(axis)
    return lax.ppermute(value, axis, [(i, i ^ bits) for i in range(size)])


def cube_gather(value, axis, steps):
    for step in steps:
        bits = lax.axis_size(axis) >> (step + 1)
        value = jnp.concatenate([value, swap(value, axis, bits)], axis=0)
    return value


def rank_slots(owners):
    slot_total = owners.shape[-1]
    earlier_mask = jnp.arange(slot_total)[None, :] < jnp.arange(slot_total)[:, None]
    same_owner = owners[..., :, None] == owners[..., None, :]
    return jnp.sum(same_owner & earlier_mask, axis=-1)


def owner_tables(all_lists, my_index, entries_here, slot_cap):
    n_seq, places = all_lists.shape
    owners = all_lists // entries_here
    ranks = rank_slots(owners)
    chosen = (owners == my_index)[:, None, :] & (
        ranks[:, None, :] == jnp.arange(slot_cap)[None, :, None]
    )

    def look(table):
        return jnp.sum(jnp.where(chosen, table[:, None, :], 0), axis=2).reshape(-1)

    def other(table):
        return table.reshape(n_seq, -1, NEIGH)[:, :, ::-1].reshape(n_seq, places)

    reader = jnp.arange(n_seq)[:, None]

    def turned(device):
        apart, position, bits = device ^ my_index, 0, n_seq >> 1
        for step in range(n_seq.bit_length() - 1):
            position = position + (apart >> step) % 2 * (bits >> step)
        return position

    partner = [
        look(other(owners)),
        look(other(ranks) + slot_cap * reader),
        look(turned(reader) + jnp.zeros_like(owners)),
        look(jnp.arange(places) + jnp.zeros_like(owners)),
        look(jnp.ones_like(owners)),
        look(turned(other(owners))),
    ]
    entry = look(all_lists % entries_here)
    return (
        jnp.repeat(entry[None], BLOCK, axis=1).astype(jnp.int32),
        jnp.stack(partner).astype(jnp.int32),
    )


def on_device(out_grad, out_weight, queries, keys, values, retrieval, counts):
    n_seq, n_mp = lax.axis_size("seq"), lax.axis_size("mp")
    my_index, my_mp = lax.axis_index("seq"), lax.axis_index("mp")
    tok_rows, head_cols = queries.shape
    entries_here, nbr_rows, _ = keys.shape
    blocks_here = tok_rows // BLOCK
    places = blocks_here * NEIGH
    slot_cap = (places + n_seq - 1) // n_seq
    rows = n_seq * slot_cap * BLOCK
    feats = out_grad.shape[1]
    lists = retrieval.T
    index_arr = my_index.astype(jnp.int32).reshape(1)
    key_rows = keys.reshape(entries_here * nbr_rows, head_cols)
    value_rows = values.reshape(entries_here * nbr_rows, head_cols)

    def exchange(slot_rows):
        cols = slot_rows.shape[-1]
        return lax.all_to_all(
            slot_rows.reshape(n_seq, slot_cap * BLOCK, cols), "seq", 0, 0, tiled=True
        ).reshape(rows, cols)

    far_bits = list(range(2, n_mp, 2))
    tie = lax.optimization_barrier
    far = [swap(out_grad, "mp", bits) for bits in far_bits]
    near = swap(out_grad, "mp", 1)
    query_places = place_rows(queries, lists, index_arr, n_seq, slot_cap, entries_here)
    query_slots = exchange(query_places)
    entry_lanes, partner = owner_tables(
        retrieval.reshape(n_seq, places), my_index, entries_here, slot_cap
    )

    placing = (lists, index_arr, n_seq, slot_cap, entries_here, HEAD_CHUNKS)
    (grad_sum,) = add_product(None, [out_grad, near], out_weight, [(my_mp, 0), (my_mp ^ 1, 0)])
    far, grad_sum = tie((far, grad_sum))
    beside = [swap(part, "mp", 1) for part in far]
    (grad_sum,) = add_product(grad_sum, far, out_weight, [(my_mp ^ bits, 0) for bits in far_bits])
    beside, grad_sum = tie((beside, grad_sum))
    grad_sum = add_product(
        grad_sum, beside, out_weight, [(my_mp ^ bits ^ 1, 0) for bits in far_bits], placing
    )
    grad_places = grad_sum

    weights, lse, seen, mean = local_softmax(query_slots, key_rows, value_rows, entry_lanes)
    grad_slots = exchange(grad_places[0])
    count_lanes = jnp.pad(counts.astype(F32), (0, LANES - blocks_here))
    count_lanes = jnp.broadcast_to(count_lanes[None], (lse.shape[0], LANES))
    all_lse = cube_gather(jnp.concatenate([lse, count_lanes], axis=1)[None], "seq", range(1))
    weights, lse, seen, mean, all_lse, partner, grad_slots = tie(
        (weights, lse, seen, mean, all_lse, partner, grad_slots)
    )
    told = row_dots(n_seq, seen, grad_slots)
    all_told = lax.all_to_all(told, "seq", 0, 0, tiled=True)
    all_lse = cube_gather(all_lse, "seq", range(1, n_seq.bit_length() - 1))
    terms = slope_terms(weights, told, grad_slots, key_rows, value_rows, entry_lanes)
    all_told, all_lse, terms = tie((all_told, all_lse, terms))
    stat, query_terms = query_terms_of(terms, mean, lse, told, all_lse, all_told, partner)
    back = exchange(query_terms).reshape(-1, BLOCK, head_cols)
    query_grad = join_places(
        0, 1, back, None, lists, index_arr, n_seq, slot_cap, entries_here, blocks_here
    )
    key_grad, value_grad = entry_grads(
        weights, stat, query_slots, grad_slots, value_rows, entry_lanes
    )
    key_grad = key_grad.reshape(keys.shape)
    value_grad = value_grad.reshape(values.shape)
    return (query_grad, key_grad, value_grad)


def solution(mesh):
    return jax.shard_map(
        on_device,
        mesh=mesh,
        in_specs=(
            P("seq", "mp"),
            P("mp", None),
            P("seq", "mp"),
            P("seq", None, "mp"),
            P("seq", None, "mp"),
            P(),
            P("seq"),
        ),
        out_specs=(P("seq", "mp"), P("seq", None, "mp"), P("seq", None, "mp")),
        check_vma=False,
    )
```
